256 devices in a mesh: dp: 8 (over z_hi, x), expert: 32 (over y, z_lo, core).
Axes of the slice: x: 4, y: 4, z: 8 (z_hi: 2, z_lo: 4; z = z_hi * 4 + z_lo), core: 2. Of those that a mesh axis runs over, the one named last changes fastest.
Arguments:
- tokens: bfloat16 [32768, 2048], P(('dp', 'expert')), may hold values from -6 to 6
- gate_weights: float32 [32768, 2], P(('dp', 'expert')), may hold values from 0.02 to 0.5
- expert_ids: int32 [32768, 2], P(('dp', 'expert')), may hold values from 0 to 31, as said below
- hot_experts: int32 [4], replicated, may hold values from 0 to 31, as said below
- gate_proj: bfloat16 [32, 2048, 768], P('expert', 'dp'), may hold values from -0.125 to 0.125
- up_proj: bfloat16 [32, 2048, 768], P('expert', 'dp'), may hold values from -0.125 to 0.125
- down_proj: bfloat16 [32, 2048, 768], P('expert', 'dp'), may hold values from -0.21875 to 0.21875
- out_grad: bfloat16 [32768, 2048], P(('dp', 'expert')), may hold values from -6 to 6
Outputs:
- layer_out: bfloat16 [32768, 2048], P(('dp', 'expert'))
- tokens_grad: bfloat16 [32768, 2048], P(('dp', 'expert'))
- routing_grad: float32 [32768, 2], P(('dp', 'expert'))
- gate_proj_grad: bfloat16 [32, 2048, 768], P('expert', 'dp')
- up_proj_grad: bfloat16 [32, 2048, 768], P('expert', 'dp')
- down_proj_grad: bfloat16 [32, 2048, 768], P('expert', 'dp')
The draws below stay inside these ranges and needn't reach their ends.
Inputs may be any that keep to these rules, and one draw needn't show every extreme that they name: `expert_ids`: each token names 2 different experts. In each block of 128 rows of one device no expert is named more than 14 times, and the expert hot_experts[0] is named exactly 14 times in every block. `hot_experts`: 4 different experts.
All inputs are finite; a program needn't handle non-finite values.
Results may differ from the reference program's by a relative error of at most 0.012.
Values may be sent and summed in bfloat16 or wider, within the bound.
A program may use at most 128 MiB of HBM per device.

```python
import math
import jax
import jax.numpy as jnp
from jax import lax

D = 2048
FF = 768
TOPK = 2
HOT = 4
TOK_DEV = 128
EXPERTS = 32
CAP = 10
SLOTS = 14
TOKENS = 32768
N_DP = 8
N_EXPERT = 32


def token_shuffle(sub_key):
    return jax.random.permutation(sub_key, TOK_DEV)


def routing_draw(key):
    blocks = TOKENS // TOK_DEV
    assigned = TOK_DEV * TOPK
    shuffled = jax.random.permutation(jax.random.fold_in(key, 17), EXPERTS).astype(jnp.int32)
    last_expert = EXPERTS - 1
    rank_index = jnp.arange(EXPERTS, dtype=jnp.int32)
    last_place = jnp.sum(jnp.where(shuffled == last_expert, rank_index, 0)).astype(jnp.int32)
    expert_order = shuffled.at[last_place].set(shuffled[1]).at[1].set(last_expert)
    remain = assigned - SLOTS
    others = EXPERTS - 1
    low_load = remain // others
    spare_count = remain % others
    high_load = low_load + min(spare_count, 1)
    reach_most = min(low_load, SLOTS - high_load)
    base_load = jnp.where(rank_index == 0, SLOTS, low_load + (rank_index - 1 < spare_count).astype(jnp.int32)).astype(jnp.int32)
    couples = others // 2
    load_moves = jax.random.randint(jax.random.fold_in(key, 23), (blocks, couples), 0, reach_most + 1, dtype=jnp.int32)
    change = jnp.zeros((blocks, EXPERTS), jnp.int32)
    change = change.at[:, 1:2 * couples:2].add(load_moves)
    change = change.at[:, 2:2 * couples + 1:2].add(-load_moves)
    ranked_load = base_load[None, :] + change
    block_loads = jnp.zeros((blocks, EXPERTS), jnp.int32).at[:, expert_order].set(ranked_load)
    load_ends = jnp.cumsum(block_loads, axis=1)
    entries = jnp.arange(assigned, dtype=jnp.int32)
    chosen = jnp.sum((load_ends[:, None, :] <= entries[None, :, None]).astype(jnp.int32), axis=2)
    id_table = jnp.transpose(chosen.reshape(blocks, TOPK, TOK_DEV), (0, 2, 1))
    token_keys = jax.random.split(jax.random.fold_in(key, 29), blocks)
    token_order = jax.vmap(token_shuffle)(token_keys).astype(jnp.int32)
    id_table = jnp.take_along_axis(id_table, token_order[:, :, None], axis=1)
    scores = jax.random.randint(jax.random.fold_in(key, 31), (blocks, TOK_DEV, TOPK), 0, 1048576, dtype=jnp.int32) * TOPK + jnp.arange(TOPK, dtype=jnp.int32)
    slot_order = jnp.argsort(scores, axis=2, stable=True).astype(jnp.int32)
    id_table = jnp.take_along_axis(id_table, slot_order, axis=2)
    return (id_table.reshape(TOKENS, TOPK).astype(jnp.int32), expert_order)


def draw_expert_ids(key, part):
    id_table, expert_order = routing_draw(key)
    return id_table


def draw_hot_experts(key, part):
    id_table, expert_order = routing_draw(key)
    pick_ranks = jnp.array([0] + [2 * member + 1 for member in range(HOT - 1)], dtype=jnp.int32)
    return expert_order[pick_ranks]


def shard_levels(stream_key, dims, pieces, least, largest):
    level, own = 1.0, jax.random.fold_in(stream_key, 6)
    for position, blocks in pieces:
        draws = jnp.exp(jax.random.uniform(jax.random.fold_in(own, position), (blocks,), jnp.float32, least / len(pieces), largest / len(pieces)))
        level = level * jnp.repeat(draws, dims[position] // blocks).reshape([-1 if axis == position else 1 for axis in range(len(dims))])
    return level


def scatter_about(own_key, extent, spread, most, shards=(), held_as=jnp.bfloat16):
    gain = shard_levels(own_key, extent, shards, -0.22, 0.18) if shards else 1.0
    drawn = jax.random.normal(own_key, extent, jnp.float32) * spread * gain
    return jnp.minimum(jnp.maximum(drawn, -most), most).astype(held_as)


def setup_inputs(seed: int = 0) -> dict:
    splits = jax.random.split(jax.random.key(seed), 9)
    return {
        "tokens": scatter_about(splits[0], (TOKENS, D), 1.0, 6.0, ((0, 256),)),
        "gate_weights": jnp.clip(jnp.exp(math.log(0.5) - 3.218876 * jax.random.uniform(splits[1], (TOKENS, TOPK), jnp.float32) ** shard_levels(splits[1], (TOKENS, TOPK), ((0, 256),), -0.2, 0.2)), 0.02, 0.5),
        "expert_ids": draw_expert_ids(jax.random.fold_in(splits[8], 71), 0),
        "hot_experts": draw_hot_experts(jax.random.fold_in(splits[8], 71), 0),
        "gate_proj": scatter_about(splits[4], (EXPERTS, D, FF), D ** -0.5, 0.125, ((0, 32), (1, 8))),
        "up_proj": scatter_about(splits[5], (EXPERTS, D, FF), D ** -0.5, 0.125, ((0, 32), (1, 8))),
        "down_proj": scatter_about(splits[6], (EXPERTS, D, FF), FF ** -0.5, 0.21875, ((0, 32), (1, 8))),
        "out_grad": scatter_about(splits[7], (TOKENS, D), 1.0, 6.0, ((0, 256),)),
    }


def split_sums(left_side, right_side):
    left_split = left_side.reshape(N_DP, -1, left_side.shape[1]).astype(jnp.float32)
    right_split = right_side.reshape(N_DP, -1, right_side.shape[1]).astype(jnp.float32)
    products = jnp.einsum("nrd,nrf->ndf", left_split, right_split, precision=lax.Precision.HIGHEST)
    rounded = lax.optimization_barrier(products.astype(jnp.bfloat16))
    return jnp.sum(rounded.astype(jnp.float32), axis=0).astype(jnp.bfloat16)


def contract_last(left_side, right_side):
    return lax.dot_general(left_side, right_side, (((1,), (1,)), ((), ())), preferred_element_type=jnp.float32)


def reference(tokens, gate_weights, expert_ids, hot_experts, gate_proj, up_proj, down_proj, out_grad):
    blocks = tokens.shape[0] // TOK_DEV
    model_width = tokens.shape[1]
    assigned = TOK_DEV * TOPK
    flat_ids = expert_ids.reshape(blocks, assigned)
    expert_range = jnp.arange(EXPERTS, dtype=jnp.int32)
    onehot = (flat_ids[:, :, None] == expert_range[None, None, :]).astype(jnp.int32)
    before = jnp.cumsum(onehot, axis=1) - onehot
    slot_pos = jnp.sum(before * onehot, axis=2)
    hot_flags = jnp.sum((hot_experts[:, None] == expert_range[None, :]).astype(jnp.int32), axis=0)
    hot_row = jnp.sum(onehot * hot_flags[None, None, :], axis=2) > 0
    kept_mask = slot_pos < jnp.where(hot_row, SLOTS, CAP)
    block_index = jnp.arange(blocks, dtype=jnp.int32)[:, None]
    token_index = block_index * TOK_DEV + jnp.arange(assigned, dtype=jnp.int32)[None, :] // TOPK
    table_size = blocks * EXPERTS * SLOTS
    target = jnp.where(kept_mask, (block_index * EXPERTS + flat_ids) * SLOTS + slot_pos, table_size)
    source_row = jnp.full((table_size + 1,), tokens.shape[0], jnp.int32).at[target.reshape(-1)].set(token_index.reshape(-1))
    source_weight = jnp.zeros((table_size + 1,), jnp.float32).at[target.reshape(-1)].set(gate_weights.reshape(-1))
    source_row = source_row[:table_size].reshape(N_DP, N_EXPERT, EXPERTS, SLOTS)
    source_weight = source_weight[:table_size].reshape(N_DP, N_EXPERT, EXPERTS, SLOTS)
    padded_tokens = jnp.concatenate([tokens, jnp.zeros((1, model_width), jnp.bfloat16)], axis=0)
    padded_grad = jnp.concatenate([out_grad, jnp.zeros((1, model_width), jnp.bfloat16)], axis=0)

    def per_expert(expert_id):
        row_ids = jnp.take(source_row, expert_id, axis=2).reshape(-1)
        row_weight = jnp.take(source_weight, expert_id, axis=2).reshape(-1, 1)
        expert_rows = padded_tokens[row_ids]
        grad_in = (row_weight * padded_grad[row_ids].astype(jnp.float32)).astype(jnp.bfloat16)
        local_gate = gate_proj[expert_id]
        local_up = up_proj[expert_id]
        local_down = down_proj[expert_id]
        gate_act = jnp.dot(expert_rows, local_gate, preferred_element_type=jnp.float32)
        up_act = jnp.dot(expert_rows, local_up, preferred_element_type=jnp.float32)
        sigmoid_act = jax.nn.sigmoid(gate_act)
        silu_act = gate_act * sigmoid_act
        hidden = (silu_act * up_act).astype(jnp.bfloat16)
        output = contract_last(hidden, local_down).astype(jnp.bfloat16)
        grad_hidden = jnp.dot(grad_in, local_down, preferred_element_type=jnp.float32)
        grad_up = (grad_hidden * silu_act).astype(jnp.bfloat16)
        grad_gate = (grad_hidden * up_act * sigmoid_act * (1.0 + gate_act * (1.0 - sigmoid_act))).astype(jnp.bfloat16)
        grad_rows = (contract_last(grad_gate, local_gate) + contract_last(grad_up, local_up)).astype(jnp.bfloat16)
        gate_sum = split_sums(expert_rows, grad_gate)
        up_sum = split_sums(expert_rows, grad_up)
        down_sum = split_sums(grad_in, hidden)
        return output, grad_rows, gate_sum, up_sum, down_sum

    outputs, grad_rows, gate_proj_grad, up_proj_grad, down_proj_grad = lax.map(per_expert, expert_range)
    dp_index = block_index // N_EXPERT
    column = block_index % N_EXPERT
    row_at = (((flat_ids * N_DP + dp_index) * N_EXPERT + column) * SLOTS + jnp.minimum(slot_pos, SLOTS - 1)).reshape(-1)
    keep_scale = kept_mask.reshape(-1, 1).astype(jnp.float32)
    chosen = jnp.take(outputs.reshape(-1, model_width), row_at, axis=0).astype(jnp.float32) * keep_scale
    weight_flat = gate_weights.reshape(-1, 1)
    layer_out = (chosen * weight_flat).reshape(-1, TOPK, model_width).sum(axis=1).astype(jnp.bfloat16)
    routing_grad = jnp.sum(chosen.reshape(-1, TOPK, model_width) * out_grad.astype(jnp.float32)[:, None, :], axis=2)
    chosen_grad = jnp.take(grad_rows.reshape(-1, model_width), row_at, axis=0).astype(jnp.float32) * keep_scale
    tokens_grad = chosen_grad.reshape(-1, TOPK, model_width).sum(axis=1).astype(jnp.bfloat16)
    return layer_out, tokens_grad, routing_grad, gate_proj_grad, up_proj_grad, down_proj_grad
```

```python
import functools

import jax
import jax.numpy as jnp
from jax import lax
from jax.experimental import pallas as pl
from jax.experimental.pallas import tpu as pltpu
from jax.sharding import PartitionSpec as P

MESH = pl.DeviceIdType.MESH
BF = jnp.bfloat16
F32 = jnp.float32
D = 2048
FF = 768
TOK = 128
NZ = 4
NQ = 8
S = 16
SH = 256
HF = SH // 2
CC = 512


def dot(a, b, ca=1, cb=0):
    return lax.dot_general(a, b, (((ca,), (cb,)), ((), ())), preferred_element_type=F32)


def kernel(
    hot_ref, ids_ref, gw_ref, tok_hbm, og_hbm, wg_hbm, wu_hbm, wd_hbm,
    lo_ref, tg_ref, rg_ref, dg_ref, du_ref, dd_ref,
    tb, ob, mb, px, pg, xr, gr, w, ga, ua, gh, hid, gg, gu, ro, rr, tp, rv, rgb, rgr,
    wgr, r2, r1, rz,
    lsem, zs, zr, ms, mr, ys, yr, vs, vr, gs, grs, ws, wr, qs, qr,
):
    d = lax.axis_index("dp")
    e = lax.axis_index("expert")
    zhi, x = d // 4, d % 4
    y, z, c = e // 8, (e // 2) % 4, e % 2
    q = y * 2 + c
    xp, xm, xo = (x + 1) % 4, (x + 3) % 4, (x + 2) % 4
    zo = 1 - zhi
    dev_xp, dev_xm = (zhi * 4 + xp, e), (zhi * 4 + xm, e)
    dev_zo = (zo * 4 + x, e)

    def dev_z(k):
        return (d, y * 8 + k * 2 + c)

    def dev_q(k):
        return (d, (k // 2) * 8 + z * 2 + k % 2)

    b1 = z - 1 + 2 * (1 - (z + 3) // 4)
    b3 = 3 * (1 - z // 2)
    b2 = 6 - z - b1 - b3
    order = (b1, b2, b3)

    barrier = pltpu.get_barrier_semaphore()
    peers = [dev_xp, dev_xm, dev_zo]
    peers += [dev_z((z + k) % NZ) for k in range(1, NZ)]
    peers += [dev_q((q + k) % NQ) for k in range(1, NQ)]
    for p in peers:
        pl.semaphore_signal(barrier, 1, device_id=p, device_id_type=MESH)
    pl.semaphore_wait(barrier, len(peers))

    def remote(src, dst, ssem, rsem, dev):
        return pltpu.make_async_remote_copy(
            src_ref=src, dst_ref=dst, send_sem=ssem, recv_sem=rsem,
            device_id=dev, device_id_type=MESH,
        )

    weights = (wg_hbm, wu_hbm, wd_hbm)

    def line_copy(a, src, buf, block, slot, target):
        return remote(src, buf.at[block], zs.at[a, slot], zr.at[a, block], dev_z(target))

    def line_start(a, hbm, buf):
        @pl.when(z < NZ - 1)
        def _():
            line_copy(a, hbm, buf, z, 0, z + 1).start()

        @pl.when(z > 0)
        def _():
            line_copy(a, hbm, buf, z, 1, z - 1).start()

    def line_step(a, buf, i):
        b = order[i]
        line_copy(a, buf.at[b], buf, b, 2, z).wait_recv()

        @pl.when((b < z) & (z < NZ - 1))
        def _():
            line_copy(a, buf.at[b], buf, b, 2 + i, z + 1).start()

        @pl.when((b > z) & (z > 0))
        def _():
            line_copy(a, buf.at[b], buf, b, 2 + i, z - 1).start()

    def line_end(a, hbm, buf):
        @pl.when(z < NZ - 1)
        def _():
            line_copy(a, hbm, buf, z, 0, z + 1).wait_send()

        @pl.when(z > 0)
        def _():
            line_copy(a, hbm, buf, z, 1, z - 1).wait_send()

        for i in range(3):
            b = order[i]

            @pl.when(((b < z) & (z < NZ - 1)) | ((b > z) & (z > 0)))
            def _(b=b, i=i):
                line_copy(a, buf.at[b], buf, b, 2 + i, z).wait_send()

    def wcopy(m, kind):
        own = weights[m]
        if kind == 0:
            return remote(own, w.at[m, x, zhi], ws.at[m, 0], wr.at[m, 0], dev_xp)
        if kind == 1:
            return remote(own, w.at[m, x, zhi], ws.at[m, 1], wr.at[m, 1], dev_xm)
        if kind == 2:
            return remote(own, w.at[m, x, zhi], ws.at[m, 2], wr.at[m, 2], dev_zo)
        g, k = (kind - 3) // 4, (kind - 3) % 4
        zh = zhi if g == 0 else zo
        sems = (ws.at[m, kind], wr.at[m, kind])
        if k == 0:
            r = w.at[m, xm, zh, pl.ds(0, HF)]
            return remote(r, r, *sems, dev_xp)
        if k == 1:
            r = w.at[m, xp, zh, pl.ds(HF, HF)]
            return remote(r, r, *sems, dev_xm)
        if k == 2:
            r = w.at[m, x, zh]
            return remote(r, r, *sems, dev_xp)
        r = w.at[m, x, zh]
        return remote(r, r, *sems, dev_xm)

    def wforward(m, g):
        first = (0, 1) if g == 0 else (9, 10)
        wcopy(m, first[0]).wait_recv()
        wcopy(m, 3 + 4 * g).start()
        wcopy(m, first[1]).wait_recv()
        wcopy(m, 4 + 4 * g).start()

    def wpartner(m):
        wcopy(m, 2).wait_recv()
        wcopy(m, 9).start()
        wcopy(m, 10).start()

    def wlast(m):
        for kind in (3, 4, 7, 8):
            wcopy(m, kind).wait_recv()

    line_start(0, tok_hbm, tb)
    for m in range(3):
        wcopy(m, 2).start()
        wcopy(m, 0).start()
        wcopy(m, 1).start()
    local = [
        pltpu.make_async_copy(tok_hbm, tb.at[z], lsem.at[0]),
        pltpu.make_async_copy(og_hbm, ob.at[z], lsem.at[1]),
    ]
    local += [pltpu.make_async_copy(weights[m], w.at[m, x, zhi], lsem.at[2 + m]) for m in range(3)]
    for cp in local:
        cp.start()

    ids0, ids1 = ids_ref[0:1, :], ids_ref[1:2, :]
    erow = lax.broadcasted_iota(jnp.int32, (32, TOK), 0)
    oh0 = (erow == ids0).astype(F32)
    oh1 = (erow == ids1).astype(F32)
    before = (
        lax.broadcasted_iota(jnp.int32, (TOK, TOK), 0)
        < lax.broadcasted_iota(jnp.int32, (TOK, TOK), 1)
    ).astype(F32)
    count = dot((oh0 + oh1).astype(BF), before.astype(BF))
    hot = (erow == hot_ref[0]) | (erow == hot_ref[1]) | (erow == hot_ref[2]) | (erow == hot_ref[3])
    room = jnp.where(hot, 14.0, 10.0)
    for k, oh, ids, here in ((0, oh0, ids0, count), (1, oh1, ids1, count + oh0)):
        slot = jnp.sum(oh * here, axis=0, keepdims=True)
        most = jnp.sum(oh * room, axis=0, keepdims=True)
        mb[z, k : k + 1, :] = jnp.where(slot < most, ids.astype(F32) * S + slot, -1.0)
        mb[z, 2 + k : 3 + k, :] = gw_ref[k : k + 1, :]
    mb[z, 4:8, :] = jnp.zeros((4, TOK), F32)

    def mcopy(k):
        return remote(mb.at[z], mb.at[z], ms.at[k], mr.at[k], dev_z((z + k) % NZ))

    for k in range(1, NZ):
        mcopy(k).start()

    def places(b):
        r = lax.broadcasted_iota(jnp.int32, (TOK, TOK), 0)
        code = ((r // 32) * 8 + z * 2 + (r // 16) % 2) * S + r % 16
        code = code.astype(F32)
        p0 = (code == mb[b, 0:1, :]).astype(F32)
        p1 = (code == mb[b, 1:2, :]).astype(F32)
        return p0, p1

    def ycopy(a, src, dst, b, k):
        return remote(src.at[(q + k) % NQ, b], dst.at[q, b], ys.at[a, k], yr.at[a, k], dev_q((q + k) % NQ))

    def ywhole(a, src, dst, k):
        return remote(src.at[(q + k) % NQ], dst.at[q], ys.at[a, k], yr.at[a, k], dev_q((q + k) % NQ))

    def pack(a, b):
        p0, p1 = places(b)
        pm = (p0 + p1).astype(BF)
        if a == 1:
            weight = jnp.sum(p0 * mb[b, 2:3, :] + p1 * mb[b, 3:4, :], axis=1, keepdims=True)
        src, dst, inp = (px, xr, tb) if a == 0 else (pg, gr, ob)

        @pl.loop(0, D // CC)
        def _(j):
            cols = pl.ds(pl.multiple_of(j * CC, CC), CC)
            rows = dot(pm, inp[b, :, cols])
            if a == 1:
                rows = rows * weight
            src[:, b, :, cols] = rows.astype(BF).reshape(NQ, S, CC)

        for k in range(1, NQ):
            ycopy(a, src, dst, b, k).start()
        dst[q, b] = src[q, b]

    local[0].wait()
    pack(0, z)
    for k in range(1, NZ):
        mcopy(k).wait_recv()
    line_step(0, tb, 0)
    pack(0, order[0])
    wforward(0, 0)
    line_step(0, tb, 1)
    pack(0, order[1])
    line_start(1, og_hbm, ob)
    wforward(1, 0)
    line_step(0, tb, 2)
    pack(0, order[2])
    wforward(2, 0)
    local[1].wait()
    pack(1, z)
    wpartner(0)
    line_step(1, ob, 0)
    pack(1, order[0])
    wpartner(1)
    line_step(1, ob, 1)
    pack(1, order[1])
    wpartner(2)
    wforward(0, 1)
    wforward(1, 1)
    line_step(1, ob, 2)
    pack(1, order[2])
    wforward(2, 1)
    for m in range(3):
        local[2 + m].wait()

    def ywait(a, src, dst):
        for k in range(1, NQ):
            ywhole(a, src, dst, k).wait_recv()

    def shard(j):
        return pl.ds(pl.multiple_of(j * SH, SH), SH)

    def rows_by(buf, j):
        return buf[:, :, :, shard(j)].reshape(NQ * NZ * S, SH)

    def through(acc, buf, m):
        acc[...] = dot(rows_by(buf, 0), w[m, 0, 0])

        @pl.loop(1, 8)
        def _(j):
            acc[...] += dot(rows_by(buf, j), w[m, j % 4, j // 4])

    ywait(0, px, xr)
    wlast(0)
    through(ga, xr, 0)
    wlast(1)
    through(ua, xr, 1)

    RB = 64

    @pl.loop(0, 512 // RB)
    def _(i):
        rs = pl.ds(pl.multiple_of(i * RB, RB), RB)
        g = ga[rs, :]
        hid[rs, :] = (g * jax.nn.sigmoid(g) * ua[rs, :]).astype(BF)

    wlast(2)
    for k in range(1, NQ):
        ywhole(0, px, xr, k).wait_send()

    @pl.loop(0, 8)
    def _(j):
        rows = dot(hid[...], w[2, j % 4, j // 4], 1, 1).astype(BF)
        px[:, :, :, shard(j)] = rows.reshape(NQ, NZ, S, SH)

    def yback(a, src, dst, k):
        t = (q + k) % NQ
        return remote(src.at[t], dst.at[q], ys.at[2 + a, k], yr.at[2 + a, k], dev_q(t))

    for k in range(1, NQ):
        yback(0, px, ro, k).start()
    ro[q] = px[q]

    ywait(1, pg, gr)
    through(gh, gr, 2)

    @pl.loop(0, 512 // RB)
    def _(i):
        rs = pl.ds(pl.multiple_of(i * RB, RB), RB)
        g, t = ga[rs, :], gh[rs, :]
        s = jax.nn.sigmoid(g)
        gu[rs, :] = (t * (g * s)).astype(BF)
        gg[rs, :] = (t * ua[rs, :] * s * (1.0 + g * (1.0 - s))).astype(BF)

    pairs = ((xr, gg), (xr, gu), (gr, hid))

    def grads(m, xx):
        left, right = pairs[m]

        @pl.loop(0, 2)
        def _(zh):
            wgr[m, xx, zh] = dot(rows_by(left, zh * 4 + xx), right[...], 0, 0).astype(BF)

    A, B = pl.ds(0, HF), pl.ds(HF, HF)

    def gcopy(m, kind):
        sems = (qs.at[m, kind], qr.at[m, kind])
        if kind == 0:
            return remote(wgr.at[m, xo, :, A], r2.at[m, 0], *sems, dev_xp)
        if kind == 1:
            return remote(wgr.at[m, xo, :, B], r2.at[m, 1], *sems, dev_xm)
        if kind == 2:
            return remote(wgr.at[m, xp, :, B], r1.at[m, 0, :, B], *sems, dev_xp)
        if kind == 3:
            return remote(wgr.at[m, xm, :, A], r1.at[m, 1, :, A], *sems, dev_xm)
        if kind == 4:
            return remote(wgr.at[m, xp, :, A], r1.at[m, 0, :, A], *sems, dev_xp)
        if kind == 5:
            return remote(wgr.at[m, xm, :, B], r1.at[m, 1, :, B], *sems, dev_xm)
        return remote(wgr.at[m, x, zo], rz.at[m], *sems, dev_zo)

    turn = (2, 0, 1)
    for m in turn:
        grads(m, xo)
        gcopy(m, 0).start()
        gcopy(m, 1).start()
    for m in turn:
        grads(m, xp)
        gcopy(m, 2).start()
        grads(m, xm)
        gcopy(m, 3).start()

    for k in range(1, NQ):
        ywhole(1, pg, gr, k).wait_send()

    @pl.loop(0, 8)
    def _(j):
        rows = dot(gg[...], w[0, j % 4, j // 4], 1, 1) + dot(gu[...], w[1, j % 4, j // 4], 1, 1)
        pg[:, :, :, shard(j)] = rows.astype(BF).reshape(NQ, NZ, S, SH)

    for k in range(1, NQ):
        yback(1, pg, rr, k).start()
    rr[q] = pg[q]
    for m in turn:
        grads(m, x)

    def merge(m):
        gcopy(m, 0).wait_recv()
        for zh in range(2):
            wgr[m, xp, zh, A] = (wgr[m, xp, zh, A].astype(F32) + r2[m, 0, zh].astype(F32)).astype(BF)
        gcopy(m, 4).start()
        gcopy(m, 1).wait_recv()
        for zh in range(2):
            wgr[m, xm, zh, B] = (wgr[m, xm, zh, B].astype(F32) + r2[m, 1, zh].astype(F32)).astype(BF)
        gcopy(m, 5).start()

    def collect(m):
        for kind in (2, 3, 4, 5):
            gcopy(m, kind).wait_recv()
        for zh in (zo, zhi):
            for half in (A, B):
                wgr[m, x, zh, half] = (
                    wgr[m, x, zh, half].astype(F32)
                    + r1[m, 0, zh, half].astype(F32)
                    + r1[m, 1, zh, half].astype(F32)
                ).astype(BF)
        gcopy(m, 6).start()

    outs = (dg_ref, du_ref, dd_ref)

    def finish(m):
        gcopy(m, 6).wait_recv()
        outs[m][...] = (wgr[m, x, zhi].astype(F32) + rz[m].astype(F32)).astype(BF)

    line_end(0, tok_hbm, tb)

    def spread(a, b):
        p0, p1 = places(b)
        src, dst = (ro, tb) if a == 0 else (rr, tp)
        if a == 0:
            pw = p0 * mb[b, 2:3, :] + p1 * mb[b, 3:4, :]
            high = pw.astype(BF)
            low = (pw - high.astype(F32)).astype(BF)

            def near(j, acc):
                cols = pl.ds(pl.multiple_of(j * CC, CC), CC)
                return acc + dot(src[:, b, :, cols].reshape(TOK, CC), ob[b, :, cols], 1, 1)

            inner = lax.fori_loop(0, D // CC, near, jnp.zeros((TOK, TOK), F32))
            rgb[b, 0:1, :] = jnp.sum(p0 * inner, axis=0, keepdims=True)
            rgb[b, 1:2, :] = jnp.sum(p1 * inner, axis=0, keepdims=True)
        else:
            high = (p0 + p1).astype(BF)

        @pl.loop(0, D // CC)
        def _(j):
            cols = pl.ds(pl.multiple_of(j * CC, CC), CC)
            rows = src[:, b, :, cols].reshape(TOK, CC)
            total = dot(high, rows, 0, 0)
            if a == 0:
                total = total + dot(low, rows, 0, 0)
            dst[b, :, cols] = total.astype(BF)

    def vright(a, t):
        buf = tb if a == 0 else tp
        return remote(buf.at[t], rv.at[a, t], vs.at[a, t], vr.at[a, t], dev_z(z + 1))

    def vleft(a, t):
        buf = tb if a == 0 else tp
        slot = jnp.where(t < z - 1, t, NZ)
        return remote(buf.at[t], rv.at[a, slot], vs.at[a, t], vr.at[a, slot], dev_z(z - 1))

    def arrived(a, slot):
        buf = tb if a == 0 else tp
        remote(buf.at[0], rv.at[a, slot], vs.at[a, 0], vr.at[a, slot], dev_z(z)).wait_recv()

    def add(a, t, slot):
        buf = tb if a == 0 else tp
        buf[t] = (buf[t].astype(F32) + rv[a, slot].astype(F32)).astype(BF)

    def vstep(a, dist):
        t = z + dist

        @pl.when(t < NZ)
        def _():
            @pl.when(z > 0)
            def _():
                arrived(a, t)
                add(a, t, t)

            vright(a, t).start()

        u = z - dist

        @pl.when(u >= 0)
        def _():
            @pl.when(z < NZ - 1)
            def _():
                arrived(a, u)
                add(a, u, u)

            vleft(a, u).start()

    def vend(a, out):
        buf = tb if a == 0 else tp

        @pl.when(z > 0)
        def _():
            arrived(a, z)
            add(a, z, z)

        @pl.when(z < NZ - 1)
        def _():
            arrived(a, NZ)
            add(a, z, NZ)

        out[...] = buf[z]

    def vsent(a):
        for dist in range(1, NZ):

            @pl.when(z + dist < NZ)
            def _(dist=dist):
                vright(a, z + dist).wait_send()

            @pl.when(z - dist >= 0)
            def _(dist=dist):
                vleft(a, z - dist).wait_send()

    def rgcopy(k):
        t = (z + k) % NZ
        return remote(rgb.at[t], rgr.at[k], gs.at[k], grs.at[k], dev_z(t))

    for b in range(NZ):
        rgb[b] = jnp.zeros((8, TOK), F32)
    for k in range(1, NQ):
        yback(0, px, ro, k).wait_recv()
    for i in (2, 1, 0):
        spread(0, order[i])
    spread(0, z)
    for k in range(1, NZ):
        rgcopy(k).start()
    vstep(0, 3)
    for m in turn:
        merge(m)
    vstep(0, 2)
    vstep(0, 1)
    for k in range(1, NQ):
        yback(1, pg, rr, k).wait_recv()
    for i in (2, 1, 0):
        spread(1, order[i])
    spread(1, z)
    vstep(1, 3)
    collect(turn[0])
    vstep(1, 2)
    vstep(1, 1)
    collect(turn[1])
    vend(0, lo_ref)
    for k in range(1, NZ):
        rgcopy(k).wait_recv()
    rg_ref[...] = (
        rgb[z, 0:2, :] + rgr[1, 0:2, :] + rgr[2, 0:2, :] + rgr[3, 0:2, :]
    )
    vend(1, tg_ref)
    collect(turn[2])
    for m in turn:
        finish(m)

    line_end(1, og_hbm, ob)
    for k in range(1, NZ):
        mcopy(k).wait_send()
        rgcopy(k).wait_send()
    for k in range(1, NQ):
        yback(0, px, ro, k).wait_send()
        yback(1, pg, rr, k).wait_send()
    vsent(0)
    vsent(1)
    for m in range(3):
        for kind in (0, 1, 2, 3, 4, 7, 8, 9, 10):
            wcopy(m, kind).wait_send()
        for kind in range(7):
            gcopy(m, kind).wait_send()


def step(tokens, gate_weights, expert_ids, hot_experts, gate_proj, up_proj, down_proj, out_grad):
    hbm = pl.BlockSpec(memory_space=pl.ANY)
    vmem = pl.BlockSpec(memory_space=pltpu.VMEM)
    smem = pl.BlockSpec(memory_space=pltpu.SMEM)
    rows4 = (NQ, NZ, S, D)
    dma = pltpu.SemaphoreType.DMA
    scratch = [
        pltpu.VMEM((NZ, TOK, D), BF),
        pltpu.VMEM((NZ, TOK, D), BF),
        pltpu.VMEM((NZ, 8, TOK), F32),
        pltpu.VMEM(rows4, BF),
        pltpu.VMEM(rows4, BF),
        pltpu.VMEM(rows4, BF),
        pltpu.VMEM(rows4, BF),
        pltpu.VMEM((3, 4, 2, SH, FF), BF),
        pltpu.VMEM((512, FF), F32),
        pltpu.VMEM((512, FF), F32),
        pltpu.VMEM((512, FF), F32),
        pltpu.VMEM((512, FF), BF),
        pltpu.VMEM((512, FF), BF),
        pltpu.VMEM((512, FF), BF),
        pltpu.VMEM(rows4, BF),
        pltpu.VMEM(rows4, BF),
        pltpu.VMEM((NZ, TOK, D), BF),
        pltpu.VMEM((2, NZ + 1, TOK, D), BF),
        pltpu.VMEM((NZ, 8, TOK), F32),
        pltpu.VMEM((NZ, 8, TOK), F32),
        pltpu.VMEM((3, 4, 2, SH, FF), BF),
        pltpu.VMEM((3, 2, 2, HF, FF), BF),
        pltpu.VMEM((3, 2, 2, SH, FF), BF),
        pltpu.VMEM((3, SH, FF), BF),
        dma((5,)),
        dma((2, 5)),
        dma((2, NZ)),
        dma((NZ,)),
        dma((NZ,)),
        dma((4, NQ)),
        dma((4, NQ)),
        dma((2, NZ)),
        dma((2, NZ + 1)),
        dma((NZ,)),
        dma((NZ,)),
        dma((3, 11)),
        dma((3, 11)),
        dma((3, 7)),
        dma((3, 7)),
    ]
    shard = jax.ShapeDtypeStruct((SH, FF), BF)
    lo, tg, rg, dg, du, dd = pl.pallas_call(
        kernel,
        out_shape=(
            jax.ShapeDtypeStruct((TOK, D), BF),
            jax.ShapeDtypeStruct((TOK, D), BF),
            jax.ShapeDtypeStruct((2, TOK), F32),
            shard,
            shard,
            shard,
        ),
        in_specs=[smem, vmem, vmem, hbm, hbm, hbm, hbm, hbm],
        out_specs=(vmem,) * 6,
        scratch_shapes=scratch,
        compiler_params=pltpu.CompilerParams(
            collective_id=0, has_side_effects=True, vmem_limit_bytes=64 << 20
        ),
    )(
        hot_experts, expert_ids.T, gate_weights.T, tokens, out_grad,
        gate_proj[0], up_proj[0], down_proj[0],
    )
    return lo, tg, rg.T, dg[None], du[None], dd[None]


def solution(mesh):
    rows = P(("dp", "expert"), None)
    mats = P("expert", "dp", None)
    return jax.shard_map(
        step,
        mesh=mesh,
        in_specs=(rows, rows, rows, P(), mats, mats, mats, rows),
        out_specs=(rows, rows, rows, mats, mats, mats),
        check_vma=False,
    )
```

```python
import jax
import jax.numpy as jnp
from jax import lax
from jax.experimental import pallas as pl
from jax.experimental.pallas import tpu as pltpu
from jax.sharding import PartitionSpec as P

MESH = pl.DeviceIdType.MESH
BF = jnp.bfloat16
F32 = jnp.float32
D = 2048
FF = 768
TOK = 128
NZ = 4
NQ = 8
S = 16
SH = 256
HF = SH // 2
CC = 512


def dot(a, b, ca=1, cb=0):
    return lax.dot_general(a, b, (((ca,), (cb,)), ((), ())), preferred_element_type=F32)


def kernel(
    hot_ref, ids_ref, gw_ref, tok_hbm, og_hbm, wg_hbm, wu_hbm, wd_hbm,
    lo_ref, tg_ref, rg_ref, dg_ref, du_ref, dd_ref,
    tb, ob, mb, px, pg, xr, gr, w, ga, ua, gh, hid, gg, gu, ro, rr, tp, rv, rgb, rgr,
    wgr, r2, r1, rz,
    lsem, zs, zr, ms, mr, ys, yr, vs, vr, gs, grs, ws, wr, qs, qr,
):
    d = lax.axis_index("dp")
    e = lax.axis_index("expert")
    zhi, x = d // 4, d % 4
    y, z, c = e // 8, (e // 2) % 4, e % 2
    q = y * 2 + c
    xp, xm, xo = (x + 1) % 4, (x + 3) % 4, (x + 2) % 4
    zo = 1 - zhi
    dev_xp, dev_xm = (zhi * 4 + xp, e), (zhi * 4 + xm, e)
    dev_zo = (zo * 4 + x, e)

    ring = zhi * 4 + z
    ahead = 1 - 2 * c

    def dev_z(k):
        p = (ring + ahead * k + 8) % 8
        return ((p // 4) * 4 + x, y * 8 + (p % 4) * 2 + c)

    def dev_q(k):
        return (d, (k // 2) * 8 + z * 2 + k % 2)

    barrier = pltpu.get_barrier_semaphore()
    peers = [dev_xp, dev_xm, dev_zo]
    peers += [dev_z(k) for k in (1, -1, 2, -2)]
    peers += [dev_q((q + k) % NQ) for k in range(1, NQ)]
    for p in peers:
        pl.semaphore_signal(barrier, 1, device_id=p, device_id_type=MESH)
    pl.semaphore_wait(barrier, len(peers))

    def remote(src, dst, ssem, rsem, dev):
        return pltpu.make_async_remote_copy(
            src_ref=src, dst_ref=dst, send_sem=ssem, recv_sem=rsem,
            device_id=dev, device_id_type=MESH,
        )

    weights = (wg_hbm, wu_hbm, wd_hbm)

    def line_copy(a, n):
        src, buf = (tok_hbm, tb) if a == 0 else (og_hbm, ob)
        if n == 3:
            return remote(buf.at[1], buf.at[3], zs.at[a, 3], zr.at[a, 3], dev_z(1))
        return remote(src, buf.at[n], zs.at[a, n], zr.at[a, n], dev_z(1 if n == 1 else -1))

    def line_start(a):
        line_copy(a, 1).start()
        line_copy(a, 2).start()

    def line_step(a, n):
        line_copy(a, n).wait_recv()
        if n == 1:
            line_copy(a, 3).start()

    def line_end(a):
        for n in (1, 2, 3):
            line_copy(a, n).wait_send()

    def wcopy(m, kind):
        own = weights[m]
        if kind == 0:
            return remote(own, w.at[m, x, zhi], ws.at[m, 0], wr.at[m, 0], dev_xp)
        if kind == 1:
            return remote(own, w.at[m, x, zhi], ws.at[m, 1], wr.at[m, 1], dev_xm)
        if kind == 2:
            return remote(own, w.at[m, x, zhi], ws.at[m, 2], wr.at[m, 2], dev_zo)
        g, k = (kind - 3) // 4, (kind - 3) % 4
        zh = zhi if g == 0 else zo
        sems = (ws.at[m, kind], wr.at[m, kind])
        if k == 0:
            r = w.at[m, xm, zh, pl.ds(0, HF)]
            return remote(r, r, *sems, dev_xp)
        if k == 1:
            r = w.at[m, xp, zh, pl.ds(HF, HF)]
            return remote(r, r, *sems, dev_xm)
        if k == 2:
            r = w.at[m, x, zh]
            return remote(r, r, *sems, dev_xp)
        r = w.at[m, x, zh]
        return remote(r, r, *sems, dev_xm)

    def wforward(m, g):
        first = (0, 1) if g == 0 else (9, 10)
        wcopy(m, first[0]).wait_recv()
        wcopy(m, 3 + 4 * g).start()
        wcopy(m, first[1]).wait_recv()
        wcopy(m, 4 + 4 * g).start()

    def wpartner(m):
        wcopy(m, 2).wait_recv()
        wcopy(m, 9).start()
        wcopy(m, 10).start()

    def wlast(m):
        for kind in (3, 4, 7, 8):
            wcopy(m, kind).wait_recv()

    line_start(0)
    for m in range(3):
        if m == 0:
            wcopy(m, 2).start()
        wcopy(m, 0).start()
        wcopy(m, 1).start()
    local = [
        pltpu.make_async_copy(tok_hbm, tb.at[0], lsem.at[0]),
        pltpu.make_async_copy(og_hbm, ob.at[0], lsem.at[1]),
    ]
    local += [pltpu.make_async_copy(weights[m], w.at[m, x, zhi], lsem.at[2 + m]) for m in range(3)]
    for cp in local:
        cp.start()

    ids0, ids1 = ids_ref[0:1, :], ids_ref[1:2, :]
    erow = lax.broadcasted_iota(jnp.int32, (32, TOK), 0)
    oh0 = (erow == ids0).astype(F32)
    oh1 = (erow == ids1).astype(F32)
    before = (
        lax.broadcasted_iota(jnp.int32, (TOK, TOK), 0)
        < lax.broadcasted_iota(jnp.int32, (TOK, TOK), 1)
    ).astype(F32)
    count = dot((oh0 + oh1).astype(BF), before.astype(BF))
    hot = (erow == hot_ref[0]) | (erow == hot_ref[1]) | (erow == hot_ref[2]) | (erow == hot_ref[3])
    room = jnp.where(hot, 14.0, 10.0)
    for k, oh, ids, here in ((0, oh0, ids0, count), (1, oh1, ids1, count + oh0)):
        slot = jnp.sum(oh * here, axis=0, keepdims=True)
        most = jnp.sum(oh * room, axis=0, keepdims=True)
        mb[0, k : k + 1, :] = jnp.where(slot < most, ids.astype(F32) * S + slot, -1.0)
        mb[0, 2 + k : 3 + k, :] = gw_ref[k : k + 1, :]
    mb[0, 4:8, :] = jnp.zeros((4, TOK), F32)

    def mcopy(k):
        return remote(mb.at[0], mb.at[k], ms.at[k], mr.at[k], dev_z((1, -1, 2)[k - 1]))

    for k in range(1, NZ):
        mcopy(k).start()

    def places(b):
        r = lax.broadcasted_iota(jnp.int32, (TOK, TOK), 0)
        code = ((r // 32) * 8 + z * 2 + (r // 16) % 2) * S + r % 16
        code = code.astype(F32)
        p0 = (code == mb[b, 0:1, :]).astype(F32)
        p1 = (code == mb[b, 1:2, :]).astype(F32)
        return p0, p1

    def ycopy(a, src, dst, b, k):
        return remote(src.at[(q + k) % NQ, b], dst.at[q, b], ys.at[a, k], yr.at[a, k], dev_q((q + k) % NQ))

    def ywhole(a, src, dst, k):
        return remote(src.at[(q + k) % NQ], dst.at[q], ys.at[a, k], yr.at[a, k], dev_q((q + k) % NQ))

    def pack(a, b):
        p0, p1 = places(b)
        pm = (p0 + p1).astype(BF)
        if a == 1:
            weight = jnp.sum(p0 * mb[b, 2:3, :] + p1 * mb[b, 3:4, :], axis=1, keepdims=True)
        src, dst, inp = (px, xr, tb) if a == 0 else (pg, gr, ob)

        @pl.loop(0, D // CC)
        def _(j):
            cols = pl.ds(pl.multiple_of(j * CC, CC), CC)
            rows = dot(pm, inp[b, :, cols])
            if a == 1:
                rows = rows * weight
            src[:, b, :, cols] = rows.astype(BF).reshape(NQ, S, CC)

        for k in range(1, NQ):
            ycopy(a, src, dst, b, k).start()
        dst[q, b] = src[q, b]

    def ywait(a, src, dst):
        for k in range(1, NQ):
            ywhole(a, src, dst, k).wait_recv()

    def shard(j):
        return pl.ds(pl.multiple_of(j * SH, SH), SH)

    def rows_by(buf, j):
        return buf[:, :, :, shard(j)].reshape(NQ * NZ * S, SH)

    def through(acc, buf, m):
        acc[...] = dot(rows_by(buf, 0), w[m, 0, 0])

        @pl.loop(1, 8)
        def _(j):
            acc[...] += dot(rows_by(buf, j), w[m, j % 4, j // 4])

    RB = 64

    def hidden_rows():
        @pl.loop(0, 512 // RB)
        def _(i):
            rs = pl.ds(pl.multiple_of(i * RB, RB), RB)
            g = ga[rs, :]
            hid[rs, :] = (g * jax.nn.sigmoid(g) * ua[rs, :]).astype(BF)

    def outputs():
        @pl.loop(0, 8)
        def _(j):
            rows = dot(hid[...], w[2, j % 4, j // 4], 1, 1).astype(BF)
            px[:, :, :, shard(j)] = rows.reshape(NQ, NZ, S, SH)

    def act_grads():
        @pl.loop(0, 512 // RB)
        def _(i):
            rs = pl.ds(pl.multiple_of(i * RB, RB), RB)
            g, t = ga[rs, :], gh[rs, :]
            s = jax.nn.sigmoid(g)
            gu[rs, :] = (t * (g * s)).astype(BF)
            gg[rs, :] = (t * ua[rs, :] * s * (1.0 + g * (1.0 - s))).astype(BF)

    def row_grads():
        @pl.loop(0, 8)
        def _(j):
            rows = dot(gg[...], w[0, j % 4, j // 4], 1, 1) + dot(gu[...], w[1, j % 4, j // 4], 1, 1)
            pg[:, :, :, shard(j)] = rows.astype(BF).reshape(NQ, NZ, S, SH)

    def yback(a, src, dst, k):
        t = (q + k) % NQ
        return remote(src.at[t], dst.at[q], ys.at[2 + a, k], yr.at[2 + a, k], dev_q(t))

    def back_start(a):
        src, dst = (px, ro) if a == 0 else (pg, rr)
        for k in range(1, NQ):
            yback(a, src, dst, k).start()
        dst[q] = src[q]

    def back_wait(a):
        src, dst = (px, ro) if a == 0 else (pg, rr)
        for k in range(1, NQ):
            yback(a, src, dst, k).wait_recv()

    def slots_sent(a):
        src, dst = (px, xr) if a == 0 else (pg, gr)
        for k in range(1, NQ):
            ywhole(a, src, dst, k).wait_send()

    pairs = ((xr, gg), (xr, gu), (gr, hid))

    def zof(i):
        return zo if i == 0 else zhi

    def grads(m, xx, i):
        left, right = pairs[m]
        wgr[m, xx, zof(i)] = dot(rows_by(left, zof(i) * 4 + xx), right[...], 0, 0).astype(BF)

    A, B = pl.ds(0, HF), pl.ds(HF, HF)

    def gcopy(m, i, kind):
        sems = (qs.at[m, i, kind], qr.at[m, i, kind])
        zh = zof(i)
        if kind == 0:
            return remote(wgr.at[m, xo, zh, A], r2.at[m, 0, i], *sems, dev_xp)
        if kind == 1:
            return remote(wgr.at[m, xo, zh, B], r2.at[m, 1, i], *sems, dev_xm)
        if kind == 2:
            return remote(wgr.at[m, xp, zh, B], r1.at[m, 0, i, B], *sems, dev_xp)
        if kind == 3:
            return remote(wgr.at[m, xm, zh, A], r1.at[m, 1, i, A], *sems, dev_xm)
        if kind == 4:
            return remote(wgr.at[m, xp, zh, A], r1.at[m, 0, i, A], *sems, dev_xp)
        if kind == 5:
            return remote(wgr.at[m, xm, zh, B], r1.at[m, 1, i, B], *sems, dev_xm)
        return remote(wgr.at[m, x, zh], rz.at[m], *sems, dev_zo)

    def scatter(m, i):
        grads(m, xo, i)
        gcopy(m, i, 0).start()
        gcopy(m, i, 1).start()
        grads(m, xp, i)
        gcopy(m, i, 2).start()
        grads(m, xm, i)
        gcopy(m, i, 3).start()

    def merge(m, i):
        zh = zof(i)
        gcopy(m, i, 0).wait_recv()
        wgr[m, xp, zh, A] = (wgr[m, xp, zh, A].astype(F32) + r2[m, 0, i].astype(F32)).astype(BF)
        gcopy(m, i, 4).start()
        gcopy(m, i, 1).wait_recv()
        wgr[m, xm, zh, B] = (wgr[m, xm, zh, B].astype(F32) + r2[m, 1, i].astype(F32)).astype(BF)
        gcopy(m, i, 5).start()

    outs = (dg_ref, du_ref, dd_ref)
    turn = (2, 0, 1)

    def collect(m):
        for kind in (2, 3, 4, 5):
            gcopy(m, 0, kind).wait_recv()
        wgr[m, x, zo] = (
            wgr[m, x, zo].astype(F32) + r1[m, 0, 0].astype(F32) + r1[m, 1, 0].astype(F32)
        ).astype(BF)
        gcopy(m, 0, 6).start()

    def finish(m):
        for kind in (2, 3, 4, 5):
            gcopy(m, 1, kind).wait_recv()
        gcopy(m, 0, 6).wait_recv()
        outs[m][...] = (
            wgr[m, x, zhi].astype(F32) + r1[m, 0, 1].astype(F32)
            + r1[m, 1, 1].astype(F32) + rz[m].astype(F32)
        ).astype(BF)

    def spread(a, b):
        p0, p1 = places(b)
        src, dst = (ro, tb) if a == 0 else (rr, tp)
        if a == 0:
            pw = p0 * mb[b, 2:3, :] + p1 * mb[b, 3:4, :]
            high = pw.astype(BF)
            low = (pw - high.astype(F32)).astype(BF)

            def near(j, acc):
                cols = pl.ds(pl.multiple_of(j * CC, CC), CC)
                return acc + dot(src[:, b, :, cols].reshape(TOK, CC), ob[b, :, cols], 1, 1)

            inner = lax.fori_loop(0, D // CC, near, jnp.zeros((TOK, TOK), F32))
            rgb[b, 2:8, :] = jnp.zeros((6, TOK), F32)
            rgb[b, 0:1, :] = jnp.sum(p0 * inner, axis=0, keepdims=True)
            rgb[b, 1:2, :] = jnp.sum(p1 * inner, axis=0, keepdims=True)
        else:
            high = (p0 + p1).astype(BF)

        @pl.loop(0, D // CC)
        def _(j):
            cols = pl.ds(pl.multiple_of(j * CC, CC), CC)
            rows = src[:, b, :, cols].reshape(TOK, CC)
            total = dot(high, rows, 0, 0)
            if a == 0:
                total = total + dot(low, rows, 0, 0)
            dst[b, :, cols] = total.astype(BF)

    def vcopy(a, n):
        buf = tb if a == 0 else tp
        slot = {3: 0, 2: 1, 1: 2}[n]
        return remote(buf.at[n], rv.at[a, slot], vs.at[a, n], vr.at[a, slot], dev_z(1 if n == 2 else -1))

    def vout(a):
        spread(a, 3)
        vcopy(a, 3).start()
        spread(a, 2)
        vcopy(a, 2).start()
        spread(a, 1)
        spread(a, 0)

    def vmerge(a):
        buf = tb if a == 0 else tp
        vcopy(a, 3).wait_recv()
        buf[1] = (buf[1].astype(F32) + rv[a, 0].astype(F32)).astype(BF)
        vcopy(a, 1).start()

    def vend(a, out):
        buf = tb if a == 0 else tp
        vcopy(a, 2).wait_recv()
        vcopy(a, 1).wait_recv()
        out[...] = (buf[0].astype(F32) + rv[a, 1].astype(F32) + rv[a, 2].astype(F32)).astype(BF)

    def rgcopy(k):
        return remote(rgb.at[k], rgr.at[k], gs.at[k], grs.at[k], dev_z((-1, 1, -2)[k - 1]))

    def rgsend():
        for k in range(1, NZ):
            rgcopy(k).start()

    def rgend():
        for k in range(1, NZ):
            rgcopy(k).wait_recv()
        rg_ref[...] = rgb[0, 0:2, :] + rgr[1, 0:2, :] + rgr[2, 0:2, :] + rgr[3, 0:2, :]

    def meta_wait():
        for k in range(1, NZ):
            mcopy(k).wait_recv()

    def local_wait(k):
        local[k].wait()

    local_wait(0)
    pack(0, 0)
    meta_wait()
    line_step(0, 1)
    wcopy(1, 2).start()
    pack(0, 1)
    line_step(0, 2)
    pack(0, 2)
    wforward(0, 0)
    line_step(0, 3)
    wcopy(2, 2).start()
    pack(0, 3)
    wforward(1, 0)
    wpartner(0)
    line_start(1)
    local_wait(1)
    pack(1, 0)
    wforward(2, 0)
    wpartner(1)
    wforward(0, 1)
    line_step(1, 1)
    pack(1, 1)
    ywait(0, px, xr)
    local_wait(2)
    wlast(0)
    through(ga, xr, 0)
    wpartner(2)
    wforward(1, 1)
    line_step(1, 2)
    pack(1, 2)
    local_wait(3)
    wlast(1)
    through(ua, xr, 1)
    hidden_rows()
    line_step(1, 3)
    pack(1, 3)
    wforward(2, 1)
    slots_sent(0)
    local_wait(4)
    wlast(2)
    outputs()
    back_start(0)
    ywait(1, pg, gr)
    scatter(2, 0)
    scatter(2, 1)
    through(gh, gr, 2)
    act_grads()
    scatter(0, 0)
    scatter(1, 0)
    slots_sent(1)
    row_grads()
    back_start(1)
    merge(2, 0)
    merge(2, 1)
    scatter(0, 1)
    scatter(1, 1)
    line_end(0)
    back_wait(0)
    vout(0)
    rgsend()
    merge(0, 0)
    merge(1, 0)
    for m in turn:
        grads(m, x, 0)
    collect(2)
    vmerge(0)
    merge(0, 1)
    merge(1, 1)
    back_wait(1)
    vout(1)
    collect(0)
    vmerge(1)
    collect(1)
    for m in turn:
        grads(m, x, 1)
    vend(0, lo_ref)
    rgend()
    vend(1, tg_ref)
    for m in turn:
        finish(m)

    line_end(1)
    for k in range(1, NZ):
        mcopy(k).wait_send()
        rgcopy(k).wait_send()
    for k in range(1, NQ):
        yback(0, px, ro, k).wait_send()
        yback(1, pg, rr, k).wait_send()
    for n in range(1, NZ):
        vcopy(0, n).wait_send()
        vcopy(1, n).wait_send()
    for m in range(3):
        for kind in (0, 1, 2, 3, 4, 7, 8, 9, 10):
            wcopy(m, kind).wait_send()
        for kind in range(7):
            gcopy(m, 0, kind).wait_send()
            if kind < 6:
                gcopy(m, 1, kind).wait_send()


def step(tokens, gate_weights, expert_ids, hot_experts, gate_proj, up_proj, down_proj, out_grad):
    hbm = pl.BlockSpec(memory_space=pl.ANY)
    vmem = pl.BlockSpec(memory_space=pltpu.VMEM)
    smem = pl.BlockSpec(memory_space=pltpu.SMEM)
    rows4 = (NQ, NZ, S, D)
    dma = pltpu.SemaphoreType.DMA
    scratch = [
        pltpu.VMEM((NZ, TOK, D), BF),
        pltpu.VMEM((NZ, TOK, D), BF),
        pltpu.VMEM((NZ, 8, TOK), F32),
        pltpu.VMEM(rows4, BF),
        pltpu.VMEM(rows4, BF),
        pltpu.VMEM(rows4, BF),
        pltpu.VMEM(rows4, BF),
        pltpu.VMEM((3, 4, 2, SH, FF), BF),
        pltpu.VMEM((512, FF), F32),
        pltpu.VMEM((512, FF), F32),
        pltpu.VMEM((512, FF), F32),
        pltpu.VMEM((512, FF), BF),
        pltpu.VMEM((512, FF), BF),
        pltpu.VMEM((512, FF), BF),
        pltpu.VMEM(rows4, BF),
        pltpu.VMEM(rows4, BF),
        pltpu.VMEM((NZ, TOK, D), BF),
        pltpu.VMEM((2, 3, TOK, D), BF),
        pltpu.VMEM((NZ, 8, TOK), F32),
        pltpu.VMEM((NZ, 8, TOK), F32),
        pltpu.VMEM((3, 4, 2, SH, FF), BF),
        pltpu.VMEM((3, 2, 2, HF, FF), BF),
        pltpu.VMEM((3, 2, 2, SH, FF), BF),
        pltpu.VMEM((3, SH, FF), BF),
        dma((5,)),
        dma((2, NZ)),
        dma((2, NZ)),
        dma((NZ,)),
        dma((NZ,)),
        dma((4, NQ)),
        dma((4, NQ)),
        dma((2, NZ)),
        dma((2, NZ)),
        dma((NZ,)),
        dma((NZ,)),
        dma((3, 11)),
        dma((3, 11)),
        dma((3, 2, 7)),
        dma((3, 2, 7)),
    ]
    shard = jax.ShapeDtypeStruct((SH, FF), BF)
    lo, tg, rg, dg, du, dd = pl.pallas_call(
        kernel,
        out_shape=(
            jax.ShapeDtypeStruct((TOK, D), BF),
            jax.ShapeDtypeStruct((TOK, D), BF),
            jax.ShapeDtypeStruct((2, TOK), F32),
            shard,
            shard,
            shard,
        ),
        in_specs=[smem, vmem, vmem, hbm, hbm, hbm, hbm, hbm],
        out_specs=(vmem,) * 6,
        scratch_shapes=scratch,
        compiler_params=pltpu.CompilerParams(
            collective_id=0, has_side_effects=True, vmem_limit_bytes=64 << 20
        ),
    )(
        hot_experts, expert_ids.T, gate_weights.T, tokens, out_grad,
        gate_proj[0], up_proj[0], down_proj[0],
    )
    return lo, tg, rg.T, dg[None], du[None], dd[None]


def solution(mesh):
    rows = P(("dp", "expert"), None)
    mats = P("expert", "dp", None)
    return jax.shard_map(
        step,
        mesh=mesh,
        in_specs=(rows, rows, rows, P(), mats, mats, mats, rows),
        out_specs=(rows, rows, rows, mats, mats, mats),
        check_vma=False,
    )
```

```python
import jax
import jax.numpy as jnp
from jax import lax
from jax.experimental import pallas as pl
from jax.experimental.pallas import tpu as pltpu
from jax.sharding import PartitionSpec as P

MESH = pl.DeviceIdType.MESH
BF = jnp.bfloat16
F32 = jnp.float32
D = 2048
FF = 768
TOK = 128
NZ = 4
NQ = 8
S = 16
SH = 256
HF = SH // 2
CC = 512


def dot(a, b, ca=1, cb=0):
    return lax.dot_general(a, b, (((ca,), (cb,)), ((), ())), preferred_element_type=F32)


def kernel(
    hot_ref, ids_ref, gw_ref, tok_hbm, og_hbm, wg_hbm, wu_hbm, wd_hbm,
    lo_ref, tg_ref, rg_ref, dg_ref, du_ref, dd_ref,
    tb, ob, mb, px, pg, xr, gr, w, ga, ua, gh, hid, gg, gu, ro, rr, tp, rv, rgb, rgr,
    wgr, r2, r1, rz,
    lsem, zs, zr, ms, mr, ys, yr, vs, vr, gs, grs, ws, wr, qs, qr,
):
    d = lax.axis_index("dp")
    e = lax.axis_index("expert")
    zhi, x = d // 4, d % 4
    y, z, c = e // 8, (e // 2) % 4, e % 2
    q = y * 2 + c
    xp, xm, xo = (x + 1) % 4, (x + 3) % 4, (x + 2) % 4
    zo = 1 - zhi
    dev_xp, dev_xm = (zhi * 4 + xp, e), (zhi * 4 + xm, e)
    dev_zo = (zo * 4 + x, e)

    ring = zhi * 4 + z
    ahead = 1 - 2 * c

    def dev_z(k):
        p = (ring + ahead * k + 8) % 8
        return ((p // 4) * 4 + x, y * 8 + (p % 4) * 2 + c)

    def dev_q(k):
        return (d, (k // 2) * 8 + z * 2 + k % 2)

    barrier = pltpu.get_barrier_semaphore()
    peers = [dev_xp, dev_xm, dev_zo]
    peers += [dev_z(k) for k in (1, -1, 2, -2)]
    peers += [dev_q((q + k) % NQ) for k in range(1, NQ)]
    for p in peers:
        pl.semaphore_signal(barrier, 1, device_id=p, device_id_type=MESH)
    pl.semaphore_wait(barrier, len(peers))

    def remote(src, dst, ssem, rsem, dev):
        return pltpu.make_async_remote_copy(
            src_ref=src, dst_ref=dst, send_sem=ssem, recv_sem=rsem,
            device_id=dev, device_id_type=MESH,
        )

    weights = (wg_hbm, wu_hbm, wd_hbm)

    def line_copy(a, n):
        src, buf = (tok_hbm, tb) if a == 0 else (og_hbm, ob)
        if n == 3:
            return remote(buf.at[1], buf.at[3], zs.at[a, 3], zr.at[a, 3], dev_z(1))
        return remote(src, buf.at[n], zs.at[a, n], zr.at[a, n], dev_z(1 if n == 1 else -1))

    def line_start(a):
        line_copy(a, 1).start()
        line_copy(a, 2).start()

    def line_step(a, n):
        line_copy(a, n).wait_recv()
        if n == 1:
            line_copy(a, 3).start()

    def line_end(a):
        for n in (1, 2, 3):
            line_copy(a, n).wait_send()

    def wcopy(m, kind):
        own = weights[m]
        if kind == 0:
            return remote(own, w.at[m, x, zhi], ws.at[m, 0], wr.at[m, 0], dev_xp)
        if kind == 1:
            return remote(own, w.at[m, x, zhi], ws.at[m, 1], wr.at[m, 1], dev_xm)
        if kind == 2:
            return remote(own, w.at[m, x, zhi], ws.at[m, 2], wr.at[m, 2], dev_zo)
        g, k = (kind - 3) // 4, (kind - 3) % 4
        zh = zhi if g == 0 else zo
        sems = (ws.at[m, kind], wr.at[m, kind])
        if k == 0:
            r = w.at[m, xm, zh, pl.ds(0, HF)]
            return remote(r, r, *sems, dev_xp)
        if k == 1:
            r = w.at[m, xp, zh, pl.ds(HF, HF)]
            return remote(r, r, *sems, dev_xm)
        if k == 2:
            r = w.at[m, x, zh]
            return remote(r, r, *sems, dev_xp)
        r = w.at[m, x, zh]
        return remote(r, r, *sems, dev_xm)

    def wforward(m, g):
        first = (0, 1) if g == 0 else (9, 10)
        wcopy(m, first[0]).wait_recv()
        wcopy(m, 3 + 4 * g).start()
        wcopy(m, first[1]).wait_recv()
        wcopy(m, 4 + 4 * g).start()

    def wpartner(m):
        wcopy(m, 2).wait_recv()
        wcopy(m, 9).start()
        wcopy(m, 10).start()

    def wlast(m):
        for kind in (3, 4, 7, 8):
            wcopy(m, kind).wait_recv()

    line_start(0)
    for m in range(3):
        if m == 0:
            wcopy(m, 2).start()
        wcopy(m, 0).start()
        wcopy(m, 1).start()
    local = [
        pltpu.make_async_copy(tok_hbm, tb.at[0], lsem.at[0]),
        pltpu.make_async_copy(og_hbm, ob.at[0], lsem.at[1]),
    ]
    local += [pltpu.make_async_copy(weights[m], w.at[m, x, zhi], lsem.at[2 + m]) for m in range(3)]
    for cp in local:
        cp.start()

    ids0, ids1 = ids_ref[0:1, :], ids_ref[1:2, :]
    erow = lax.broadcasted_iota(jnp.int32, (32, TOK), 0)
    oh0 = (erow == ids0).astype(F32)
    oh1 = (erow == ids1).astype(F32)
    before = (
        lax.broadcasted_iota(jnp.int32, (TOK, TOK), 0)
        < lax.broadcasted_iota(jnp.int32, (TOK, TOK), 1)
    ).astype(F32)
    count = dot((oh0 + oh1).astype(BF), before.astype(BF))
    hot = (erow == hot_ref[0]) | (erow == hot_ref[1]) | (erow == hot_ref[2]) | (erow == hot_ref[3])
    room = jnp.where(hot, 14.0, 10.0)
    for k, oh, ids, here in ((0, oh0, ids0, count), (1, oh1, ids1, count + oh0)):
        slot = jnp.sum(oh * here, axis=0, keepdims=True)
        most = jnp.sum(oh * room, axis=0, keepdims=True)
        mb[0, k : k + 1, :] = jnp.where(slot < most, ids.astype(F32) * S + slot, -1.0)
        mb[0, 2 + k : 3 + k, :] = gw_ref[k : k + 1, :]
    mb[0, 4:8, :] = jnp.zeros((4, TOK), F32)

    def mcopy(k):
        return remote(mb.at[0], mb.at[k], ms.at[k], mr.at[k], dev_z((1, -1, 2)[k - 1]))

    for k in range(1, NZ):
        mcopy(k).start()

    def places(b):
        r = lax.broadcasted_iota(jnp.int32, (TOK, TOK), 0)
        code = ((r // 32) * 8 + z * 2 + (r // 16) % 2) * S + r % 16
        code = code.astype(F32)
        p0 = (code == mb[b, 0:1, :]).astype(F32)
        p1 = (code == mb[b, 1:2, :]).astype(F32)
        return p0, p1

    def ycopy(a, src, dst, b, k):
        return remote(src.at[(q + k) % NQ, b], dst.at[q, b], ys.at[a, k], yr.at[a, k], dev_q((q + k) % NQ))

    def ywhole(a, src, dst, k):
        return remote(src.at[(q + k) % NQ], dst.at[q], ys.at[a, k], yr.at[a, k], dev_q((q + k) % NQ))

    def pack(a, b):
        p0, p1 = places(b)
        pm = (p0 + p1).astype(BF)
        if a == 1:
            weight = jnp.sum(p0 * mb[b, 2:3, :] + p1 * mb[b, 3:4, :], axis=1, keepdims=True)
        src, dst, inp = (px, xr, tb) if a == 0 else (pg, gr, ob)

        @pl.loop(0, D // CC)
        def _(j):
            cols = pl.ds(pl.multiple_of(j * CC, CC), CC)
            rows = dot(pm, inp[b, :, cols])
            if a == 1:
                rows = rows * weight
            src[:, b, :, cols] = rows.astype(BF).reshape(NQ, S, CC)

        for k in range(1, NQ):
            ycopy(a, src, dst, b, k).start()
        dst[q, b] = src[q, b]

    def ywait(a, src, dst):
        for k in range(1, NQ):
            ywhole(a, src, dst, k).wait_recv()

    def shard(j):
        return pl.ds(pl.multiple_of(j * SH, SH), SH)

    def rows_by(buf, j):
        return buf[:, :, :, shard(j)].reshape(NQ * NZ * S, SH)

    def through(acc, buf, m):
        acc[...] = dot(rows_by(buf, 0), w[m, 0, 0])

        @pl.loop(1, 8)
        def _(j):
            acc[...] += dot(rows_by(buf, j), w[m, j % 4, j // 4])

    RB = 64

    def hidden_rows():
        @pl.loop(0, 512 // RB)
        def _(i):
            rs = pl.ds(pl.multiple_of(i * RB, RB), RB)
            g = ga[rs, :]
            hid[rs, :] = (g * jax.nn.sigmoid(g) * ua[rs, :]).astype(BF)

    def outputs():
        @pl.loop(0, 8)
        def _(j):
            rows = dot(hid[...], w[2, j % 4, j // 4], 1, 1).astype(BF)
            px[:, :, :, shard(j)] = rows.reshape(NQ, NZ, S, SH)

    def act_grads():
        @pl.loop(0, 512 // RB)
        def _(i):
            rs = pl.ds(pl.multiple_of(i * RB, RB), RB)
            g, t = ga[rs, :], gh[rs, :]
            s = jax.nn.sigmoid(g)
            gu[rs, :] = (t * (g * s)).astype(BF)
            gg[rs, :] = (t * ua[rs, :] * s * (1.0 + g * (1.0 - s))).astype(BF)

    def row_grads():
        @pl.loop(0, 8)
        def _(j):
            rows = dot(gg[...], w[0, j % 4, j // 4], 1, 1) + dot(gu[...], w[1, j % 4, j // 4], 1, 1)
            pg[:, :, :, shard(j)] = rows.astype(BF).reshape(NQ, NZ, S, SH)

    def yback(a, src, dst, k):
        t = (q + k) % NQ
        return remote(src.at[t], dst.at[q], ys.at[2 + a, k], yr.at[2 + a, k], dev_q(t))

    def back_start(a):
        src, dst = (px, ro) if a == 0 else (pg, rr)
        for k in range(1, NQ):
            yback(a, src, dst, k).start()
        dst[q] = src[q]

    def back_wait(a):
        src, dst = (px, ro) if a == 0 else (pg, rr)
        for k in range(1, NQ):
            yback(a, src, dst, k).wait_recv()

    def slots_sent(a):
        src, dst = (px, xr) if a == 0 else (pg, gr)
        for k in range(1, NQ):
            ywhole(a, src, dst, k).wait_send()

    pairs = ((xr, gg), (xr, gu), (gr, hid))

    def zof(i):
        return zo if i == 0 else zhi

    def grads(m, xx, i):
        left, right = pairs[m]
        wgr[m, xx, zof(i)] = dot(rows_by(left, zof(i) * 4 + xx), right[...], 0, 0).astype(BF)

    A, B = pl.ds(0, HF), pl.ds(HF, HF)

    def gcopy(m, i, kind):
        sems = (qs.at[m, i, kind], qr.at[m, i, kind])
        zh = zof(i)
        if kind == 0:
            return remote(wgr.at[m, xo, zh, A], r2.at[m, 0, i], *sems, dev_xp)
        if kind == 1:
            return remote(wgr.at[m, xo, zh, B], r2.at[m, 1, i], *sems, dev_xm)
        if kind == 2:
            return remote(wgr.at[m, xp, zh, B], r1.at[m, 0, i, B], *sems, dev_xp)
        if kind == 3:
            return remote(wgr.at[m, xm, zh, A], r1.at[m, 1, i, A], *sems, dev_xm)
        if kind == 4:
            return remote(wgr.at[m, xp, zh, A], r1.at[m, 0, i, A], *sems, dev_xp)
        if kind == 5:
            return remote(wgr.at[m, xm, zh, B], r1.at[m, 1, i, B], *sems, dev_xm)
        return remote(wgr.at[m, x, zh], rz.at[m], *sems, dev_zo)

    def scatter(m, i):
        grads(m, xo, i)
        gcopy(m, i, 0).start()
        gcopy(m, i, 1).start()
        grads(m, xp, i)
        gcopy(m, i, 2).start()
        grads(m, xm, i)
        gcopy(m, i, 3).start()

    def merge(m, i):
        zh = zof(i)
        gcopy(m, i, 0).wait_recv()
        wgr[m, xp, zh, A] = (wgr[m, xp, zh, A].astype(F32) + r2[m, 0, i].astype(F32)).astype(BF)
        gcopy(m, i, 4).start()
        gcopy(m, i, 1).wait_recv()
        wgr[m, xm, zh, B] = (wgr[m, xm, zh, B].astype(F32) + r2[m, 1, i].astype(F32)).astype(BF)
        gcopy(m, i, 5).start()

    outs = (dg_ref, du_ref, dd_ref)
    turn = (2, 0, 1)

    def collect(m):
        for kind in (2, 3, 4, 5):
            gcopy(m, 0, kind).wait_recv()
        wgr[m, x, zo] = (
            wgr[m, x, zo].astype(F32) + r1[m, 0, 0].astype(F32) + r1[m, 1, 0].astype(F32)
        ).astype(BF)
        gcopy(m, 0, 6).start()

    def finish(m):
        for kind in (2, 3, 4, 5):
            gcopy(m, 1, kind).wait_recv()
        gcopy(m, 0, 6).wait_recv()
        outs[m][...] = (
            wgr[m, x, zhi].astype(F32) + r1[m, 0, 1].astype(F32)
            + r1[m, 1, 1].astype(F32) + rz[m].astype(F32)
        ).astype(BF)

    def spread(a, b):
        p0, p1 = places(b)
        src, dst = (ro, tb) if a == 0 else (rr, tp)
        if a == 0:

            def near(j, acc):
                cols = pl.ds(pl.multiple_of(j * CC, CC), CC)
                return acc + dot(src[:, b, :, cols].reshape(TOK, CC), ob[b, :, cols], 1, 1)

            inner = lax.fori_loop(0, D // CC, near, jnp.zeros((TOK, TOK), F32))
            rgb[b, 2:8, :] = jnp.zeros((6, TOK), F32)
            rgb[b, 0:1, :] = jnp.sum(p0 * inner, axis=0, keepdims=True)
            rgb[b, 1:2, :] = jnp.sum(p1 * inner, axis=0, keepdims=True)
            pw = jnp.transpose(p0 * mb[b, 2:3, :] + p1 * mb[b, 3:4, :])
            high = pw.astype(BF)
            mix = jnp.concatenate([high, (pw - high.astype(F32)).astype(BF)], axis=1)
        else:
            mix = jnp.transpose(p0 + p1).astype(BF)

        @pl.loop(0, D // CC)
        def _(j):
            cols = pl.ds(pl.multiple_of(j * CC, CC), CC)
            rows = src[:, b, :, cols].reshape(TOK, CC)
            if a == 0:
                rows = jnp.concatenate([rows, rows], axis=0)
            dst[b, :, cols] = dot(mix, rows).astype(BF)

    def vcopy(a, n):
        buf = tb if a == 0 else tp
        slot = {3: 0, 2: 1, 1: 2}[n]
        return remote(buf.at[n], rv.at[a, slot], vs.at[a, n], vr.at[a, slot], dev_z(1 if n == 2 else -1))

    def vout(a):
        spread(a, 3)
        vcopy(a, 3).start()
        spread(a, 2)
        vcopy(a, 2).start()
        spread(a, 1)
        spread(a, 0)

    def vmerge(a):
        buf = tb if a == 0 else tp
        vcopy(a, 3).wait_recv()
        buf[1] = (buf[1].astype(F32) + rv[a, 0].astype(F32)).astype(BF)
        vcopy(a, 1).start()

    def vend(a, out):
        buf = tb if a == 0 else tp
        vcopy(a, 2).wait_recv()
        vcopy(a, 1).wait_recv()
        out[...] = (buf[0].astype(F32) + rv[a, 1].astype(F32) + rv[a, 2].astype(F32)).astype(BF)

    def rgcopy(k):
        return remote(rgb.at[k], rgr.at[k], gs.at[k], grs.at[k], dev_z((-1, 1, -2)[k - 1]))

    def rgsend():
        for k in range(1, NZ):
            rgcopy(k).start()

    def rgend():
        for k in range(1, NZ):
            rgcopy(k).wait_recv()
        rg_ref[...] = rgb[0, 0:2, :] + rgr[1, 0:2, :] + rgr[2, 0:2, :] + rgr[3, 0:2, :]

    def meta_wait():
        for k in range(1, NZ):
            mcopy(k).wait_recv()

    def local_wait(k):
        local[k].wait()

    local_wait(0)
    pack(0, 0)
    meta_wait()
    line_step(0, 1)
    pack(0, 1)
    line_step(0, 2)
    wcopy(1, 2).start()
    pack(0, 2)
    wforward(0, 0)
    line_step(0, 3)
    pack(0, 3)
    wpartner(0)
    line_start(1)
    wforward(1, 0)
    wforward(2, 0)
    local_wait(1)
    pack(1, 0)
    wpartner(1)
    wcopy(2, 2).start()
    wforward(0, 1)
    ywait(0, px, xr)
    local_wait(2)
    wlast(0)
    through(ga, xr, 0)
    wforward(1, 1)
    line_step(1, 1)
    pack(1, 1)
    wpartner(2)
    local_wait(3)
    wlast(1)
    through(ua, xr, 1)
    hidden_rows()
    line_step(1, 2)
    pack(1, 2)
    line_step(1, 3)
    pack(1, 3)
    wforward(2, 1)
    ywait(1, pg, gr)
    scatter(2, 0)
    slots_sent(0)
    local_wait(4)
    wlast(2)
    outputs()
    back_start(0)
    through(gh, gr, 2)
    act_grads()
    scatter(0, 0)
    merge(2, 0)
    scatter(1, 0)
    slots_sent(1)
    row_grads()
    back_start(1)
    grads(2, x, 0)
    merge(0, 0)
    merge(1, 0)
    collect(2)
    scatter(2, 1)
    line_end(0)
    back_wait(0)
    vout(0)
    rgsend()
    scatter(0, 1)
    merge(2, 1)
    grads(0, x, 0)
    collect(0)
    scatter(1, 1)
    grads(1, x, 0)
    collect(1)
    merge(0, 1)
    merge(1, 1)
    vmerge(0)
    back_wait(1)
    vout(1)
    for m in turn:
        grads(m, x, 1)
    vmerge(1)
    vend(0, lo_ref)
    rgend()
    finish(2)
    vend(1, tg_ref)
    finish(0)
    finish(1)

    line_end(1)
    for k in range(1, NZ):
        mcopy(k).wait_send()
        rgcopy(k).wait_send()
    for k in range(1, NQ):
        yback(0, px, ro, k).wait_send()
        yback(1, pg, rr, k).wait_send()
    for n in range(1, NZ):
        vcopy(0, n).wait_send()
        vcopy(1, n).wait_send()
    for m in range(3):
        for kind in (0, 1, 2, 3, 4, 7, 8, 9, 10):
            wcopy(m, kind).wait_send()
        for kind in range(7):
            gcopy(m, 0, kind).wait_send()
            if kind < 6:
                gcopy(m, 1, kind).wait_send()


def step(tokens, gate_weights, expert_ids, hot_experts, gate_proj, up_proj, down_proj, out_grad):
    hbm = pl.BlockSpec(memory_space=pl.ANY)
    vmem = pl.BlockSpec(memory_space=pltpu.VMEM)
    smem = pl.BlockSpec(memory_space=pltpu.SMEM)
    rows4 = (NQ, NZ, S, D)
    dma = pltpu.SemaphoreType.DMA
    scratch = [
        pltpu.VMEM((NZ, TOK, D), BF),
        pltpu.VMEM((NZ, TOK, D), BF),
        pltpu.VMEM((NZ, 8, TOK), F32),
        pltpu.VMEM(rows4, BF),
        pltpu.VMEM(rows4, BF),
        pltpu.VMEM(rows4, BF),
        pltpu.VMEM(rows4, BF),
        pltpu.VMEM((3, 4, 2, SH, FF), BF),
        pltpu.VMEM((512, FF), F32),
        pltpu.VMEM((512, FF), F32),
        pltpu.VMEM((512, FF), F32),
        pltpu.VMEM((512, FF), BF),
        pltpu.VMEM((512, FF), BF),
        pltpu.VMEM((512, FF), BF),
        pltpu.VMEM(rows4, BF),
        pltpu.VMEM(rows4, BF),
        pltpu.VMEM((NZ, TOK, D), BF),
        pltpu.VMEM((2, 3, TOK, D), BF),
        pltpu.VMEM((NZ, 8, TOK), F32),
        pltpu.VMEM((NZ, 8, TOK), F32),
        pltpu.VMEM((3, 4, 2, SH, FF), BF),
        pltpu.VMEM((3, 2, 2, HF, FF), BF),
        pltpu.VMEM((3, 2, 2, SH, FF), BF),
        pltpu.VMEM((3, SH, FF), BF),
        dma((5,)),
        dma((2, NZ)),
        dma((2, NZ)),
        dma((NZ,)),
        dma((NZ,)),
        dma((4, NQ)),
        dma((4, NQ)),
        dma((2, NZ)),
        dma((2, NZ)),
        dma((NZ,)),
        dma((NZ,)),
        dma((3, 11)),
        dma((3, 11)),
        dma((3, 2, 7)),
        dma((3, 2, 7)),
    ]
    shard = jax.ShapeDtypeStruct((SH, FF), BF)
    lo, tg, rg, dg, du, dd = pl.pallas_call(
        kernel,
        out_shape=(
            jax.ShapeDtypeStruct((TOK, D), BF),
            jax.ShapeDtypeStruct((TOK, D), BF),
            jax.ShapeDtypeStruct((2, TOK), F32),
            shard,
            shard,
            shard,
        ),
        in_specs=[smem, vmem, vmem, hbm, hbm, hbm, hbm, hbm],
        out_specs=(vmem,) * 6,
        scratch_shapes=scratch,
        compiler_params=pltpu.CompilerParams(
            collective_id=0, has_side_effects=True, vmem_limit_bytes=64 << 20
        ),
    )(
        hot_experts, expert_ids.T, gate_weights.T, tokens, out_grad,
        gate_proj[0], up_proj[0], down_proj[0],
    )
    return lo, tg, rg.T, dg[None], du[None], dd[None]


def solution(mesh):
    rows = P(("dp", "expert"), None)
    mats = P("expert", "dp", None)
    return jax.shard_map(
        step,
        mesh=mesh,
        in_specs=(rows, rows, rows, P(), mats, mats, mats, rows),
        out_specs=(rows, rows, rows, mats, mats, mats),
        check_vma=False,
    )
```

```python
import jax
import jax.numpy as jnp
from jax import lax
from jax.experimental import pallas as pl
from jax.experimental.pallas import tpu as pltpu
from jax.sharding import PartitionSpec as P

MESH = pl.DeviceIdType.MESH
BF = jnp.bfloat16
F32 = jnp.float32
D = 2048
FF = 768
TOK = 128
NZ = 4
NQ = 8
S = 16
SH = 256
HF = SH // 2
CC = 512


def dot(a, b, ca=1, cb=0):
    return lax.dot_general(a, b, (((ca,), (cb,)), ((), ())), preferred_element_type=F32)


def kernel(
    hot_ref, ids_ref, gw_ref, tok_hbm, og_hbm, wg_hbm, wu_hbm, wd_hbm,
    lo_ref, tg_ref, rg_ref, dg_ref, du_ref, dd_ref,
    tb, ob, mb, px, pg, xr, gr, w, ga, ua, gh, hid, gg, gu, ro, rr, tp, rv, rgb, rgr,
    wgr, r2, r1, rz,
    lsem, zs, zr, ms, mr, ys, yr, vs, vr, gs, grs, ws, wr, qs, qr,
):
    d = lax.axis_index("dp")
    e = lax.axis_index("expert")
    zhi, x = d // 4, d % 4
    y, z, c = e // 8, (e // 2) % 4, e % 2
    q = y * 2 + c
    xp, xm, xo = (x + 1) % 4, (x + 3) % 4, (x + 2) % 4
    zo = 1 - zhi
    dev_xp, dev_xm = (zhi * 4 + xp, e), (zhi * 4 + xm, e)
    dev_zo = (zo * 4 + x, e)

    ring = zhi * 4 + z
    ahead = 1 - 2 * c

    def dev_z(k):
        p = (ring + ahead * k + 8) % 8
        return ((p // 4) * 4 + x, y * 8 + (p % 4) * 2 + c)

    def dev_q(k):
        return (d, (k // 2) * 8 + z * 2 + k % 2)

    barrier = pltpu.get_barrier_semaphore()
    peers = [dev_xp, dev_xm, dev_zo]
    peers += [dev_z(k) for k in (1, -1, 2, -2)]
    peers += [dev_q((q + k) % NQ) for k in range(1, NQ)]
    for p in peers:
        pl.semaphore_signal(barrier, 1, device_id=p, device_id_type=MESH)
    pl.semaphore_wait(barrier, len(peers))

    def remote(src, dst, ssem, rsem, dev):
        return pltpu.make_async_remote_copy(
            src_ref=src, dst_ref=dst, send_sem=ssem, recv_sem=rsem,
            device_id=dev, device_id_type=MESH,
        )

    weights = (wg_hbm, wu_hbm, wd_hbm)

    def line_copy(a, n):
        src, buf = (tok_hbm, tb) if a == 0 else (og_hbm, ob)
        if n == 3:
            return remote(buf.at[1], buf.at[3], zs.at[a, 3], zr.at[a, 3], dev_z(1))
        return remote(src, buf.at[n], zs.at[a, n], zr.at[a, n], dev_z(1 if n == 1 else -1))

    def line_start(a):
        line_copy(a, 1).start()
        line_copy(a, 2).start()

    def line_step(a, n):
        line_copy(a, n).wait_recv()
        if n == 1:
            line_copy(a, 3).start()

    def line_end(a):
        for n in (1, 2, 3):
            line_copy(a, n).wait_send()

    def wcopy(m, kind):
        own = weights[m]
        if kind == 0:
            return remote(own, w.at[m, x, zhi], ws.at[m, 0], wr.at[m, 0], dev_xp)
        if kind == 1:
            return remote(own, w.at[m, x, zhi], ws.at[m, 1], wr.at[m, 1], dev_xm)
        if kind == 2:
            return remote(own, w.at[m, x, zhi], ws.at[m, 2], wr.at[m, 2], dev_zo)
        g, k = (kind - 3) // 4, (kind - 3) % 4
        zh = zhi if g == 0 else zo
        sems = (ws.at[m, kind], wr.at[m, kind])
        if k == 0:
            r = w.at[m, xm, zh, pl.ds(0, HF)]
            return remote(r, r, *sems, dev_xp)
        if k == 1:
            r = w.at[m, xp, zh, pl.ds(HF, HF)]
            return remote(r, r, *sems, dev_xm)
        if k == 2:
            r = w.at[m, x, zh]
            return remote(r, r, *sems, dev_xp)
        r = w.at[m, x, zh]
        return remote(r, r, *sems, dev_xm)

    def wforward(m, g):
        first = (0, 1) if g == 0 else (9, 10)
        wcopy(m, first[0]).wait_recv()
        wcopy(m, 3 + 4 * g).start()
        wcopy(m, first[1]).wait_recv()
        wcopy(m, 4 + 4 * g).start()

    def wpartner(m):
        wcopy(m, 2).wait_recv()
        wcopy(m, 9).start()
        wcopy(m, 10).start()

    def wlast(m):
        for kind in (3, 4, 7, 8):
            wcopy(m, kind).wait_recv()

    line_start(0)
    for m in range(3):
        if m == 0:
            wcopy(m, 2).start()
        wcopy(m, 0).start()
        wcopy(m, 1).start()
    local = [
        pltpu.make_async_copy(tok_hbm, tb.at[0], lsem.at[0]),
        pltpu.make_async_copy(og_hbm, ob.at[0], lsem.at[1]),
    ]
    local += [pltpu.make_async_copy(weights[m], w.at[m, x, zhi], lsem.at[2 + m]) for m in range(3)]
    for cp in local:
        cp.start()

    ids0, ids1 = ids_ref[0:1, :], ids_ref[1:2, :]
    erow = lax.broadcasted_iota(jnp.int32, (32, TOK), 0)
    oh0 = (erow == ids0).astype(F32)
    oh1 = (erow == ids1).astype(F32)
    before = (
        lax.broadcasted_iota(jnp.int32, (TOK, TOK), 0)
        < lax.broadcasted_iota(jnp.int32, (TOK, TOK), 1)
    ).astype(F32)
    count = dot((oh0 + oh1).astype(BF), before.astype(BF))
    hot = (erow == hot_ref[0]) | (erow == hot_ref[1]) | (erow == hot_ref[2]) | (erow == hot_ref[3])
    room = jnp.where(hot, 14.0, 10.0)
    for k, oh, ids, here in ((0, oh0, ids0, count), (1, oh1, ids1, count + oh0)):
        slot = jnp.sum(oh * here, axis=0, keepdims=True)
        most = jnp.sum(oh * room, axis=0, keepdims=True)
        mb[0, k : k + 1, :] = jnp.where(slot < most, ids.astype(F32) * S + slot, -1.0)
        mb[0, 2 + k : 3 + k, :] = gw_ref[k : k + 1, :]
    mb[0, 4:8, :] = jnp.zeros((4, TOK), F32)

    def mcopy(k):
        return remote(mb.at[0], mb.at[k], ms.at[k], mr.at[k], dev_z((1, -1, 2)[k - 1]))

    for k in range(1, NZ):
        mcopy(k).start()

    def places(b):
        r = lax.broadcasted_iota(jnp.int32, (TOK, TOK), 0)
        code = ((r // 32) * 8 + z * 2 + (r // 16) % 2) * S + r % 16
        code = code.astype(F32)
        p0 = (code == mb[b, 0:1, :]).astype(F32)
        p1 = (code == mb[b, 1:2, :]).astype(F32)
        return p0, p1

    def ycopy(a, src, dst, b, k):
        return remote(src.at[(q + k) % NQ, b], dst.at[q, b], ys.at[a, k], yr.at[a, k], dev_q((q + k) % NQ))

    def ywhole(a, src, dst, k):
        return remote(src.at[(q + k) % NQ], dst.at[q], ys.at[a, k], yr.at[a, k], dev_q((q + k) % NQ))

    def pack(a, b):
        p0, p1 = places(b)
        pm = (p0 + p1).astype(BF)
        if a == 1:
            weight = jnp.sum(p0 * mb[b, 2:3, :] + p1 * mb[b, 3:4, :], axis=1, keepdims=True)
        src, dst, inp = (px, xr, tb) if a == 0 else (pg, gr, ob)

        @pl.loop(0, D // CC)
        def _(j):
            cols = pl.ds(pl.multiple_of(j * CC, CC), CC)
            rows = dot(pm, inp[b, :, cols])
            if a == 1:
                rows = rows * weight
            src[:, b, :, cols] = rows.astype(BF).reshape(NQ, S, CC)

        for k in range(1, NQ):
            ycopy(a, src, dst, b, k).start()
        dst[q, b] = src[q, b]

    def ywait(a, src, dst):
        for k in range(1, NQ):
            ywhole(a, src, dst, k).wait_recv()

    def shard(j):
        return pl.ds(pl.multiple_of(j * SH, SH), SH)

    def rows_by(buf, j):
        return buf[:, :, :, shard(j)].reshape(NQ * NZ * S, SH)

    def through(acc, buf, m):
        acc[...] = dot(rows_by(buf, 0), w[m, 0, 0])

        @pl.loop(1, 8)
        def _(j):
            acc[...] += dot(rows_by(buf, j), w[m, j % 4, j // 4])

    RB = 64

    def hidden_rows():
        @pl.loop(0, 512 // RB)
        def _(i):
            rs = pl.ds(pl.multiple_of(i * RB, RB), RB)
            g = ga[rs, :]
            hid[rs, :] = (g * jax.nn.sigmoid(g) * ua[rs, :]).astype(BF)

    def outputs():
        @pl.loop(0, 8)
        def _(j):
            rows = dot(hid[...], w[2, j % 4, j // 4], 1, 1).astype(BF)
            px[:, :, :, shard(j)] = rows.reshape(NQ, NZ, S, SH)

    def act_grads():
        @pl.loop(0, 512 // RB)
        def _(i):
            rs = pl.ds(pl.multiple_of(i * RB, RB), RB)
            g, t = ga[rs, :], gh[rs, :]
            s = jax.nn.sigmoid(g)
            gu[rs, :] = (t * (g * s)).astype(BF)
            gg[rs, :] = (t * ua[rs, :] * s * (1.0 + g * (1.0 - s))).astype(BF)

    def row_grads():
        @pl.loop(0, 8)
        def _(j):
            rows = dot(gg[...], w[0, j % 4, j // 4], 1, 1) + dot(gu[...], w[1, j % 4, j // 4], 1, 1)
            pg[:, :, :, shard(j)] = rows.astype(BF).reshape(NQ, NZ, S, SH)

    def yback(a, src, dst, k):
        t = (q + k) % NQ
        return remote(src.at[t], dst.at[q], ys.at[2 + a, k], yr.at[2 + a, k], dev_q(t))

    def back_start(a):
        src, dst = (px, ro) if a == 0 else (pg, rr)
        for k in range(1, NQ):
            yback(a, src, dst, k).start()
        dst[q] = src[q]

    def back_wait(a):
        src, dst = (px, ro) if a == 0 else (pg, rr)
        for k in range(1, NQ):
            yback(a, src, dst, k).wait_recv()

    def slots_sent(a):
        src, dst = (px, xr) if a == 0 else (pg, gr)
        for k in range(1, NQ):
            ywhole(a, src, dst, k).wait_send()

    pairs = ((xr, gg), (xr, gu), (gr, hid))

    def zof(i):
        return zo if i == 0 else zhi

    def grads(m, xx, i):
        left, right = pairs[m]
        wgr[m, xx, zof(i)] = dot(rows_by(left, zof(i) * 4 + xx), right[...], 0, 0).astype(BF)

    A, B = pl.ds(0, HF), pl.ds(HF, HF)

    def gcopy(m, i, kind):
        sems = (qs.at[m, i, kind], qr.at[m, i, kind])
        zh = zof(i)
        if kind == 0:
            return remote(wgr.at[m, xo, zh, A], r2.at[m, 0, i], *sems, dev_xp)
        if kind == 1:
            return remote(wgr.at[m, xo, zh, B], r2.at[m, 1, i], *sems, dev_xm)
        if kind == 2:
            return remote(wgr.at[m, xp, zh, B], r1.at[m, 0, i, B], *sems, dev_xp)
        if kind == 3:
            return remote(wgr.at[m, xm, zh, A], r1.at[m, 1, i, A], *sems, dev_xm)
        if kind == 4:
            return remote(wgr.at[m, xp, zh, A], r1.at[m, 0, i, A], *sems, dev_xp)
        if kind == 5:
            return remote(wgr.at[m, xm, zh, B], r1.at[m, 1, i, B], *sems, dev_xm)
        return remote(wgr.at[m, x, zh], rz.at[m], *sems, dev_zo)

    def scatter(m, i):
        grads(m, xo, i)
        gcopy(m, i, 0).start()
        gcopy(m, i, 1).start()
        grads(m, xp, i)
        gcopy(m, i, 2).start()
        grads(m, xm, i)
        gcopy(m, i, 3).start()

    def merge(m, i):
        zh = zof(i)
        gcopy(m, i, 0).wait_recv()
        wgr[m, xp, zh, A] = (wgr[m, xp, zh, A].astype(F32) + r2[m, 0, i].astype(F32)).astype(BF)
        gcopy(m, i, 4).start()
        gcopy(m, i, 1).wait_recv()
        wgr[m, xm, zh, B] = (wgr[m, xm, zh, B].astype(F32) + r2[m, 1, i].astype(F32)).astype(BF)
        gcopy(m, i, 5).start()

    outs = (dg_ref, du_ref, dd_ref)
    turn = (2, 0, 1)

    def collect(m):
        for kind in (2, 3, 4, 5):
            gcopy(m, 0, kind).wait_recv()
        wgr[m, x, zo] = (
            wgr[m, x, zo].astype(F32) + r1[m, 0, 0].astype(F32) + r1[m, 1, 0].astype(F32)
        ).astype(BF)
        gcopy(m, 0, 6).start()

    def finish(m):
        for kind in (2, 3, 4, 5):
            gcopy(m, 1, kind).wait_recv()
        gcopy(m, 0, 6).wait_recv()
        outs[m][...] = (
            wgr[m, x, zhi].astype(F32) + r1[m, 0, 1].astype(F32)
            + r1[m, 1, 1].astype(F32) + rz[m].astype(F32)
        ).astype(BF)

    def spread(a, b):
        p0, p1 = places(b)
        src, dst = (ro, tb) if a == 0 else (rr, tp)
        if a == 0:

            def near(j, acc):
                cols = pl.ds(pl.multiple_of(j * CC, CC), CC)
                return acc + dot(src[:, b, :, cols].reshape(TOK, CC), ob[b, :, cols], 1, 1)

            inner = lax.fori_loop(0, D // CC, near, jnp.zeros((TOK, TOK), F32))
            rgb[b, 2:8, :] = jnp.zeros((6, TOK), F32)
            rgb[b, 0:1, :] = jnp.sum(p0 * inner, axis=0, keepdims=True)
            rgb[b, 1:2, :] = jnp.sum(p1 * inner, axis=0, keepdims=True)
            pw = jnp.transpose(p0 * mb[b, 2:3, :] + p1 * mb[b, 3:4, :])
            high = pw.astype(BF)
            mix = jnp.concatenate([high, (pw - high.astype(F32)).astype(BF)], axis=1)
        else:
            mix = jnp.transpose(p0 + p1).astype(BF)

        @pl.loop(0, D // CC)
        def _(j):
            cols = pl.ds(pl.multiple_of(j * CC, CC), CC)
            rows = src[:, b, :, cols].reshape(TOK, CC)
            if a == 0:
                rows = jnp.concatenate([rows, rows], axis=0)
            dst[b, :, cols] = dot(mix, rows).astype(BF)

    def vcopy(a, n):
        buf = tb if a == 0 else tp
        slot = {3: 0, 2: 1, 1: 2}[n]
        return remote(buf.at[n], rv.at[a, slot], vs.at[a, n], vr.at[a, slot], dev_z(1 if n == 2 else -1))

    def vout(a):
        spread(a, 3)
        vcopy(a, 3).start()
        spread(a, 2)
        vcopy(a, 2).start()
        spread(a, 1)
        spread(a, 0)

    def vmerge(a):
        buf = tb if a == 0 else tp
        vcopy(a, 3).wait_recv()
        buf[1] = (buf[1].astype(F32) + rv[a, 0].astype(F32)).astype(BF)
        vcopy(a, 1).start()

    def vend(a, out):
        buf = tb if a == 0 else tp
        vcopy(a, 2).wait_recv()
        vcopy(a, 1).wait_recv()
        out[...] = (buf[0].astype(F32) + rv[a, 1].astype(F32) + rv[a, 2].astype(F32)).astype(BF)

    def rgcopy(k):
        return remote(rgb.at[k], rgr.at[k], gs.at[k], grs.at[k], dev_z((-1, 1, -2)[k - 1]))

    def rgsend():
        for k in range(1, NZ):
            rgcopy(k).start()

    def rgend():
        for k in range(1, NZ):
            rgcopy(k).wait_recv()
        rg_ref[...] = rgb[0, 0:2, :] + rgr[1, 0:2, :] + rgr[2, 0:2, :] + rgr[3, 0:2, :]

    def meta_wait():
        for k in range(1, NZ):
            mcopy(k).wait_recv()

    def local_wait(k):
        local[k].wait()

    local_wait(0)
    pack(0, 0)
    meta_wait()
    line_step(0, 1)
    pack(0, 1)
    line_step(0, 2)
    wcopy(1, 2).start()
    pack(0, 2)
    wforward(0, 0)
    line_step(0, 3)
    pack(0, 3)
    wpartner(0)
    line_start(1)
    wforward(1, 0)
    wforward(2, 0)
    local_wait(1)
    pack(1, 0)
    wpartner(1)
    wcopy(2, 2).start()
    wforward(0, 1)
    ywait(0, px, xr)
    local_wait(2)
    wlast(0)
    through(ga, xr, 0)
    wforward(1, 1)
    line_step(1, 1)
    pack(1, 1)
    wpartner(2)
    local_wait(3)
    wlast(1)
    through(ua, xr, 1)
    hidden_rows()
    line_step(1, 2)
    pack(1, 2)
    line_step(1, 3)
    pack(1, 3)
    wforward(2, 1)
    ywait(1, pg, gr)
    scatter(2, 0)
    slots_sent(0)
    local_wait(4)
    wlast(2)
    through(gh, gr, 2)
    act_grads()
    scatter(0, 0)
    merge(2, 0)
    scatter(1, 0)
    outputs()
    back_start(0)
    grads(2, x, 0)
    collect(2)
    slots_sent(1)
    row_grads()
    back_start(1)
    merge(0, 0)
    merge(1, 0)
    scatter(2, 1)
    line_end(0)
    back_wait(0)
    vout(0)
    rgsend()
    scatter(0, 1)
    merge(2, 1)
    grads(0, x, 0)
    collect(0)
    scatter(1, 1)
    grads(1, x, 0)
    collect(1)
    merge(0, 1)
    merge(1, 1)
    vmerge(0)
    back_wait(1)
    vout(1)
    for m in turn:
        grads(m, x, 1)
    vmerge(1)
    vend(0, lo_ref)
    rgend()
    finish(2)
    vend(1, tg_ref)
    finish(0)
    finish(1)

    line_end(1)
    for k in range(1, NZ):
        mcopy(k).wait_send()
        rgcopy(k).wait_send()
    for k in range(1, NQ):
        yback(0, px, ro, k).wait_send()
        yback(1, pg, rr, k).wait_send()
    for n in range(1, NZ):
        vcopy(0, n).wait_send()
        vcopy(1, n).wait_send()
    for m in range(3):
        for kind in (0, 1, 2, 3, 4, 7, 8, 9, 10):
            wcopy(m, kind).wait_send()
        for kind in range(7):
            gcopy(m, 0, kind).wait_send()
            if kind < 6:
                gcopy(m, 1, kind).wait_send()


def step(tokens, gate_weights, expert_ids, hot_experts, gate_proj, up_proj, down_proj, out_grad):
    hbm = pl.BlockSpec(memory_space=pl.ANY)
    vmem = pl.BlockSpec(memory_space=pltpu.VMEM)
    smem = pl.BlockSpec(memory_space=pltpu.SMEM)
    rows4 = (NQ, NZ, S, D)
    dma = pltpu.SemaphoreType.DMA
    scratch = [
        pltpu.VMEM((NZ, TOK, D), BF),
        pltpu.VMEM((NZ, TOK, D), BF),
        pltpu.VMEM((NZ, 8, TOK), F32),
        pltpu.VMEM(rows4, BF),
        pltpu.VMEM(rows4, BF),
        pltpu.VMEM(rows4, BF),
        pltpu.VMEM(rows4, BF),
        pltpu.VMEM((3, 4, 2, SH, FF), BF),
        pltpu.VMEM((512, FF), F32),
        pltpu.VMEM((512, FF), F32),
        pltpu.VMEM((512, FF), F32),
        pltpu.VMEM((512, FF), BF),
        pltpu.VMEM((512, FF), BF),
        pltpu.VMEM((512, FF), BF),
        pltpu.VMEM(rows4, BF),
        pltpu.VMEM(rows4, BF),
        pltpu.VMEM((NZ, TOK, D), BF),
        pltpu.VMEM((2, 3, TOK, D), BF),
        pltpu.VMEM((NZ, 8, TOK), F32),
        pltpu.VMEM((NZ, 8, TOK), F32),
        pltpu.VMEM((3, 4, 2, SH, FF), BF),
        pltpu.VMEM((3, 2, 2, HF, FF), BF),
        pltpu.VMEM((3, 2, 2, SH, FF), BF),
        pltpu.VMEM((3, SH, FF), BF),
        dma((5,)),
        dma((2, NZ)),
        dma((2, NZ)),
        dma((NZ,)),
        dma((NZ,)),
        dma((4, NQ)),
        dma((4, NQ)),
        dma((2, NZ)),
        dma((2, NZ)),
        dma((NZ,)),
        dma((NZ,)),
        dma((3, 11)),
        dma((3, 11)),
        dma((3, 2, 7)),
        dma((3, 2, 7)),
    ]
    shard = jax.ShapeDtypeStruct((SH, FF), BF)
    lo, tg, rg, dg, du, dd = pl.pallas_call(
        kernel,
        out_shape=(
            jax.ShapeDtypeStruct((TOK, D), BF),
            jax.ShapeDtypeStruct((TOK, D), BF),
            jax.ShapeDtypeStruct((2, TOK), F32),
            shard,
            shard,
            shard,
        ),
        in_specs=[smem, vmem, vmem, hbm, hbm, hbm, hbm, hbm],
        out_specs=(vmem,) * 6,
        scratch_shapes=scratch,
        compiler_params=pltpu.CompilerParams(
            collective_id=0, has_side_effects=True, vmem_limit_bytes=64 << 20
        ),
    )(
        hot_experts, expert_ids.T, gate_weights.T, tokens, out_grad,
        gate_proj[0], up_proj[0], down_proj[0],
    )
    return lo, tg, rg.T, dg[None], du[None], dd[None]


def solution(mesh):
    rows = P(("dp", "expert"), None)
    mats = P("expert", "dp", None)
    return jax.shard_map(
        step,
        mesh=mesh,
        in_specs=(rows, rows, rows, P(), mats, mats, mats, rows),
        out_specs=(rows, rows, rows, mats, mats, mats),
        check_vma=False,
    )
```
